256 devices in a mesh: tm: 4 (over z_hi, core), space: 64 (over x, y, z_lo).
Axes of the slice: x: 4, y: 4, z: 8 (z_hi: 2, z_lo: 4; z = z_hi * 4 + z_lo), core: 2. Of those that a mesh axis runs over, the one named last changes fastest.
Arguments:
- grain_labels: int32 [256, 16, 256], P('space'), may hold values from 0 to 127
- particle_mask: int32 [256, 16, 256], P('space'), may hold values 0 or 1
- grain_class: int32 [128], replicated, may hold values from 0 to 3
- class_energy: float32 [4], replicated, may hold values from 0.1 to 1
Outputs:
- slice_start: float32 [4, 8, 256, 16, 256], P('tm', None, 'space')
- slice_end: float32 [4, 8, 256, 16, 256], P('tm', None, 'space')
The draws below stay inside these ranges and needn't reach their ends.
All inputs are finite; a program needn't handle non-finite values. No bound on the sum of `particle_mask` on one device may be relied on, other than what follows from the above.
Results may differ from the reference program's by a relative error of at most 0.0001.
Values sent between devices are 32-bit elements; how exact they have to be, the bound alone decides.
A program may use at most 64 MiB of HBM per device.

```python
import math
import jax
import jax.numpy as jnp

ORDERS = 8
NGRAIN = 128
NCLASS = 4
FINE = 2
ITERS = 2
SLICES = 4
NX = 256
NZ = 16
NY = 256


def with_ends(result, rng, low, largest):
    longest = result.shape.index(max(result.shape))
    spots = []
    for shift in (0, 1):
        where = [jax.random.randint(jax.random.fold_in(rng, axis), (), 0, length) for axis, length in enumerate(result.shape)]
        where[longest] = (where[longest] + shift) % result.shape[longest]
        spots.append(tuple(where))
    return result.at[spots[0]].set(low).at[spots[1]].set(largest)


def setup_inputs(seed: int = 0) -> dict:
    arg_keys = jax.random.split(jax.random.key(seed), 5)
    return {
        "grain_labels": with_ends(jax.random.randint(arg_keys[0], (NX, NZ, NY), 0, NGRAIN), jax.random.fold_in(arg_keys[0], 1), 0, NGRAIN - 1).astype(jnp.int32),
        "particle_mask": with_ends((jax.random.randint(arg_keys[1], (NX, NZ, NY), 0, 5) < 1).astype(jnp.int32), jax.random.fold_in(arg_keys[1], 1), 0, 1),
        "grain_class": with_ends(jax.random.randint(arg_keys[2], (NGRAIN,), 0, NCLASS), jax.random.fold_in(arg_keys[2], 1), 0, NCLASS - 1).astype(jnp.int32),
        "class_energy": jnp.clip(jnp.exp(jax.random.uniform(arg_keys[3], (NCLASS,), jnp.float32, math.log(0.1), math.log(1.0))), 0.1, 1.0),
    }


fine_dt = 0.06


def coefficients(labels, particles, grain_class, class_energy):
    grain_energy = class_energy[grain_class]
    stored = grain_energy[labels]
    orders = jnp.arange(ORDERS, dtype=jnp.int32)[:, None, None, None]
    own = ((labels[None] % ORDERS) == orders).astype(jnp.float32)
    drive = stored[None] * own
    mobility = 1.0 - 0.75 * particles.astype(jnp.float32)
    return own, drive, mobility


def evolve(center, xplus, xminus, drive, mobility, step_size):
    beside = xplus + xminus + jnp.roll(center, -1, 2) + jnp.roll(center, 1, 2)
    beside = beside + jnp.roll(center, -1, 3) + jnp.roll(center, 1, 3)
    laplace = beside - 6.0 * center
    squares = center * center
    total = jnp.sum(squares, axis=0, keepdims=True)
    force = squares * center - center + 3.0 * center * (total - squares) - laplace + drive * center
    return center - step_size * mobility[None] * force


def advance(field, drive, mobility, step_size):
    return evolve(field, jnp.roll(field, -1, 1), jnp.roll(field, 1, 1), drive, mobility, step_size)


def reference(grain_labels, particle_mask, grain_class, class_energy):
    own, drive, mobility = coefficients(grain_labels, particle_mask, grain_class, class_energy)
    coarse_dt = fine_dt * FINE

    def coarse(field):
        return advance(field, drive, mobility, coarse_dt)

    def fine(field):
        for inner in range(FINE):
            field = advance(field, drive, mobility, fine_dt)
        return field

    starts = []
    coarse_vals = []
    current = own
    for slot in range(SLICES):
        starts.append(current)
        value = coarse(current)
        coarse_vals.append(value)
        current = value
    ends = list(coarse_vals)
    for sweep in range(ITERS):
        jumps = [fine(starts[slot]) - coarse_vals[slot] for slot in range(SLICES)]
        new_starts = []
        current = own
        for slot in range(SLICES):
            new_starts.append(current)
            value = coarse(current)
            coarse_vals[slot] = value
            ending = value + jumps[slot]
            ends[slot] = ending
            current = ending
        starts = new_starts
    return jnp.stack(starts), jnp.stack(ends)
```

```python
import functools
import math

import jax
import jax.numpy as jnp
from jax import lax
from jax.experimental import pallas as pl
from jax.experimental.pallas import tpu as pltpu
from jax.sharding import PartitionSpec as P

MESH = pl.DeviceIdType.MESH
ORDERS = 8
HALO = 6
ROWS = 4
EXT = ROWS + 2 * HALO
FINE_DT = 0.06
ROOT2 = math.sqrt(2.0)

NEEDED = {
    "u0": (1, 3, 4, 5),
    "u0p": (0, 2, 3, 4),
    "c1": (-1, -1, 3, 4),
    "c1p": (-1, -1, 2, 3),
    "a1": (-1, 1, 2, 3),
    "a1p": (-1, 0, 1, 2),
    "c2": (-1, -1, -1, 3),
    "c2p": (-1, -1, -1, 2),
    "b2": (-1, -1, 1, 2),
    "b2p": (-1, -1, 0, 1),
    "a2": (-1, -1, 0, 1),
    "b3": (-1, -1, -1, 1),
    "b3p": (-1, -1, -1, 0),
    "d3": (-1, -1, -1, 0),
}


def by_slice(tm, values):
    result = jnp.int32(values[0])
    for index in range(1, len(values)):
        result = jnp.where(tm >= index, jnp.int32(values[index]), result)
    return result


def exchange_kernel(lab_ref, msk_ref, lab_ext, msk_ext, local_sem, send_sem, recv_sem):
    tm, me = lax.axis_index("tm"), lax.axis_index("space")
    count = lax.axis_size("space")
    place = lax.rem(me, 4)

    def partner(distance):
        crossed = jnp.where(jnp.logical_or(place + distance < 0, place + distance > 3), 1, 0)
        half = lax.rem(tm // 2 + crossed, 2)
        return (half * 2 + lax.rem(tm, 2), lax.rem(me + distance + count, count))

    barrier = pltpu.get_barrier_semaphore()
    for distance in (-2, -1, 1, 2):
        pl.semaphore_signal(barrier, inc=1, device_id=partner(distance), device_id_type=MESH)
    own = [
        pltpu.make_async_copy(src, dst.at[pl.ds(HALO, ROWS)], local_sem.at[k])
        for k, (src, dst) in enumerate(((lab_ref, lab_ext), (msk_ref, msk_ext)))
    ]
    for copy in own:
        copy.start()
    pl.semaphore_wait(barrier, 4)
    moves = ((1, 0, 4, 2), (-1, 0, 4, 10), (2, 2, 2, 0), (-2, 0, 2, 14))
    copies = []
    for m, (distance, first, rows, there) in enumerate(moves):
        for k, (src, dst) in enumerate(((lab_ref, lab_ext), (msk_ref, msk_ext))):
            copies.append(
                pltpu.make_async_remote_copy(
                    src_ref=src.at[pl.ds(first, rows)],
                    dst_ref=dst.at[pl.ds(there, rows)],
                    send_sem=send_sem.at[2 * m + k],
                    recv_sem=recv_sem.at[2 * m + k],
                    device_id=partner(distance),
                    device_id_type=MESH,
                )
            )
    for copy in copies:
        copy.start()
    for copy in own:
        copy.wait()
    for copy in copies:
        copy.wait()


def exchange(labels, particles):
    shape = jax.ShapeDtypeStruct((EXT,) + labels.shape[1:], jnp.int32)
    return pl.pallas_call(
        exchange_kernel,
        out_shape=(shape, shape),
        in_specs=[pl.BlockSpec(memory_space=pl.ANY)] * 2,
        out_specs=[pl.BlockSpec(memory_space=pl.ANY)] * 2,
        scratch_shapes=[
            pltpu.SemaphoreType.DMA((2,)),
            pltpu.SemaphoreType.DMA((8,)),
            pltpu.SemaphoreType.DMA((8,)),
        ],
        compiler_params=pltpu.CompilerParams(collective_id=0, has_side_effects=True),
        name="exchange",
    )(labels, particles)


def lanes(shape=(8, 128)):
    return lax.broadcasted_iota(jnp.int32, shape, 1)


def pick(x, index):
    return jnp.take_along_axis(x, index, axis=1, mode="promise_in_bounds")


def apart(ref, row, zt, yt):
    low = ref[0, row, pl.ds(zt, 8, stride=2), :]
    high = ref[1, row, pl.ds(zt, 8, stride=2), :]
    index = lax.rem(2 * lanes() + yt, 128)
    return jnp.where(lanes() < 64, pick(low, index), pick(high, index))


def together(out, order, row, tiles):
    odd = lax.rem(lanes(), 2) == 1
    for zt in (0, 1):
        for half in (0, 1):
            index = lanes() // 2 + 64 * half
            mixed = jnp.where(odd, pick(tiles[2 * zt + 1], index), pick(tiles[2 * zt], index))
            out[half, order, row, pl.ds(zt, 8, stride=2), :] = mixed


def neighbours(ref, row, order):
    e = [ref[row, tile, order] for tile in range(4)]
    odd, even = e[1] + e[2], e[0] + e[3]
    beside = [
        odd + pltpu.roll(e[1], 1, 1) + pltpu.roll(e[2], 1, 0),
        even + pltpu.roll(e[0], 127, 1) + pltpu.roll(e[3], 1, 0),
        even + pltpu.roll(e[3], 1, 1) + pltpu.roll(e[0], 7, 0),
        odd + pltpu.roll(e[2], 127, 1) + pltpu.roll(e[1], 7, 0),
    ]
    total = [beside[tile] + (ref[row - 1, tile, order] + ref[row + 1, tile, order]) for tile in range(4)]
    return e, total


def annealing_kernel(
    lab_hbm, msk_hbm, class_ref, energy_ref, start_hbm, end_hbm,
    lab_ref, msk_ref, start_ref, end_ref, in_sem, out_sem, rate, drive, pinned, u0, u0p, c1, a1, c1p, c2, jump1, a1p, b2, c2p, jump2, b2p, b3, a2, jump3, d3, b3p, jump4, e4,
):
    tm = lax.axis_index("tm")

    copies = []
    for k, (src, dst) in enumerate(((lab_hbm, lab_ref), (msk_hbm, msk_ref))):
        for half in (0, 1):
            copies.append(pltpu.make_async_copy(src.at[:, :, pl.ds(128 * half, 128)], dst.at[half], in_sem.at[2 * k + half]))
    for copy in copies:
        copy.start()
    for copy in copies:
        copy.wait()

    classes = jnp.broadcast_to(class_ref[...], (8, 128))
    table = jnp.full((8, 128), energy_ref[0], jnp.float32)
    for kind in range(1, 4):
        table = jnp.where(classes == kind, energy_ref[kind], table)

    def prepare(row, carry):
        for tile in range(4):
            label = apart(lab_ref, row, tile // 2, tile % 2)
            particle = apart(msk_ref, row, tile // 2, tile % 2).astype(jnp.float32)
            rate[row, tile] = FINE_DT - (0.75 * FINE_DT) * particle
            stored = pick(table, label)
            center = (ROOT2 * 6.0) + ROOT2 * stored
            order = lax.rem(label, ORDERS)
            for p in range(ORDERS):
                mine = order == p
                u0[row, tile, p] = jnp.where(mine, ROOT2, 0.0)
                drive[row, tile, p] = jnp.where(mine, stored, 0.0)
                pinned[row, tile, p] = jnp.where(mine, center, 0.0)
        return carry

    lax.fori_loop(0, EXT, prepare, 0)

    def rows(name, body):
        reach = by_slice(tm, NEEDED[name])
        def once(row, carry):
            body(row)
            return carry
        lax.fori_loop(HALO - reach, jnp.where(reach < 0, HALO - reach, HALO + ROWS + reach), once, 0)

    def force(name, field, store):
        def body(row):
            squares = [[None] * ORDERS for _ in range(4)]
            level = []
            for tile in range(4):
                total = None
                for p in range(ORDERS):
                    center = field[row, tile, p]
                    squares[tile][p] = center * center
                    total = squares[tile][p] if total is None else total + squares[tile][p]
                level.append(1.5 * total + 5.0)
            speed = [rate[row, tile] for tile in range(4)]
            for p in range(ORDERS):
                e, beside = neighbours(field, row, p)
                for tile in range(4):
                    slope = squares[tile][p] - (level[tile] + drive[row, tile, p])
                    store(row, tile, p, e[tile], speed[tile] * (beside[tile] + e[tile] * slope))
        rows(name, body)

    def first(row):
        speed = [rate[row, tile] for tile in range(4)]
        for p in range(ORDERS):
            e, beside = neighbours(u0, row, p)
            for tile in range(4):
                change = speed[tile] * (beside[tile] - pinned[row, tile, p])
                half = e[tile] + change
                u0p[row, tile, p] = half
                c1[row, tile, p] = half + change

    rows("u0", first)

    def to_a1(row, tile, p, e, change):
        a1[row, tile, p] = e + change

    def to_c2(row, tile, p, e, change):
        half = e + change
        c1p[row, tile, p] = half
        c2[row, tile, p] = half + change
        jump1[row, tile, p] = change

    def to_jump1(row, tile, p, e, change):
        jump1[row, tile, p] = change - jump1[row, tile, p]

    def to_b2(row, tile, p, e, change):
        half = e + change
        a1p[row, tile, p] = half
        b2[row, tile, p] = half + (change + jump1[row, tile, p])

    def to_c2p(row, tile, p, e, change):
        c2p[row, tile, p] = e + change
        jump2[row, tile, p] = change

    def to_jump2(row, tile, p, e, change):
        jump2[row, tile, p] = change - jump2[row, tile, p]

    def to_b3(row, tile, p, e, change):
        half = e + change
        b2p[row, tile, p] = half
        b3[row, tile, p] = half + (change + jump2[row, tile, p])
        jump3[row, tile, p] = change

    def to_a2(row, tile, p, e, change):
        a2[row, tile, p] = e + change

    def to_jump3(row, tile, p, e, change):
        jump3[row, tile, p] = change - jump3[row, tile, p]

    def to_d3(row, tile, p, e, change):
        d3[row, tile, p] = (e + change) + (change + jump3[row, tile, p])

    def to_b3p(row, tile, p, e, change):
        b3p[row, tile, p] = e + change
        jump4[row, tile, p] = change

    def to_jump4(row, tile, p, e, change):
        jump4[row, tile, p] = change - jump4[row, tile, p]

    def to_e4(row, tile, p, e, change):
        e4[row, tile, p] = (e + change) + (change + jump4[row, tile, p])

    force("u0p", u0p, to_a1)
    force("c1", c1, to_c2)
    force("c1p", c1p, to_jump1)
    force("a1", a1, to_b2)
    force("a1p", a1p, to_a2)
    force("c2", c2, to_c2p)
    force("c2p", c2p, to_jump2)
    force("b2", b2, to_b3)
    force("b2p", b2p, to_jump3)
    force("a2", a2, to_d3)
    force("b3", b3, to_b3p)
    force("b3p", b3p, to_jump4)
    force("d3", d3, to_e4)

    def write(out, field):
        def once(row, carry):
            for p in range(ORDERS):
                tiles = [field[row + HALO, tile, p] * (1.0 / ROOT2) for tile in range(4)]
                together(out, p, row, tiles)
            return carry
        lax.fori_loop(0, ROWS, once, 0)

    results = (u0, a1, a2, d3, e4)
    for index in range(4):
        @pl.when(tm == index)
        def _():
            write(start_ref, results[index])
            write(end_ref, results[index + 1])

    copies = []
    for k, (src, dst) in enumerate(((start_ref, start_hbm), (end_ref, end_hbm))):
        for half in (0, 1):
            copies.append(pltpu.make_async_copy(src.at[half], dst.at[0, :, :, :, pl.ds(128 * half, 128)], out_sem.at[2 * k + half]))
    for copy in copies:
        copy.start()
    for copy in copies:
        copy.wait()


def annealing(lab_ext, msk_ext, grain_class, class_energy):
    out = jax.ShapeDtypeStruct((1, ORDERS, ROWS, 16, 256), jnp.float32)
    tiles = lambda *extra: pltpu.VMEM((EXT, 4) + extra + (8, 128), jnp.float32)
    return pl.pallas_call(
        annealing_kernel,
        out_shape=(out, out),
        in_specs=[pl.BlockSpec(memory_space=pl.ANY)] * 2
        + [pl.BlockSpec(memory_space=pltpu.VMEM), pl.BlockSpec(memory_space=pltpu.SMEM)],
        out_specs=[pl.BlockSpec(memory_space=pl.ANY)] * 2,
        scratch_shapes=[pltpu.VMEM((2, EXT, 16, 128), jnp.int32)] * 2
        + [pltpu.VMEM((2, ORDERS, ROWS, 16, 128), jnp.float32)] * 2
        + [pltpu.SemaphoreType.DMA((4,)), pltpu.SemaphoreType.DMA((4,))]
        + [tiles()]
        + [tiles(ORDERS)] * 21,
        compiler_params=pltpu.CompilerParams(vmem_limit_bytes=60 * 1024 * 1024),
        name="annealing",
    )(lab_ext, msk_ext, grain_class.reshape(1, -1), class_energy)


def local(grain_labels, particle_mask, grain_class, class_energy):
    lab_ext, msk_ext = exchange(grain_labels, particle_mask)
    return annealing(lab_ext, msk_ext, grain_class, class_energy)


def solution(mesh):
    placed = (P("space", None, None), P("space", None, None), P(), P())
    return jax.shard_map(
        local,
        mesh=mesh,
        in_specs=placed,
        out_specs=(P("tm", None, "space", None, None), P("tm", None, "space", None, None)),
        check_vma=False,
    )
```

```python
import functools
import math

import jax
import jax.numpy as jnp
from jax import lax
from jax.experimental import pallas as pl
from jax.experimental.pallas import tpu as pltpu
from jax.sharding import PartitionSpec as P

MESH = pl.DeviceIdType.MESH
ORDERS = 8
HALO = 6
ROWS = 4
EXT = ROWS + 2 * HALO
FINE_DT = 0.06
ROOT2 = math.sqrt(2.0)

REACH = {
    "1": (1, 3, 4, 5),
    "2": (0, 2, 3, 4),
    "3": (-1, 1, 2, 3),
    "4": (-1, 0, 1, 2),
    "5": (-1, -1, 0, 1),
    "6": (-1, -1, -1, 0),
}


def by_slice(tm, values):
    result = jnp.int32(values[0])
    for index in range(1, len(values)):
        result = jnp.where(tm >= index, jnp.int32(values[index]), result)
    return result


TURN = (1, 127)


def order_of_lanes(across):
    y = lax.broadcasted_iota(jnp.int32, (256, 256), across)
    place = lax.broadcasted_iota(jnp.int32, (256, 256), 1 - across)
    return jnp.where(y == 2 * (place & 127) + (place >> 7), 1.0, 0.0).astype(jnp.bfloat16)


class View:
    def __init__(self, store, first, orders):
        self.store, self.first, self.orders = store, first, orders

    def at(self, index):
        return (index[0], self.first + index[1] * self.orders + (index[2] if self.orders > 1 else 0))

    def __getitem__(self, index):
        return self.store[self.at(index)]

    def __setitem__(self, index, tile):
        self.store[self.at(index)] = tile

    def brick(self, tile):
        return self.store[pl.ds(HALO, ROWS), pl.ds(self.first + tile * self.orders, self.orders)]


class Shelf:
    def __init__(self, store):
        self.store, self.used = store, 0

    def planes(self):
        return self.view(1)

    def field(self):
        return self.view(ORDERS)

    def view(self, orders):
        self.used += 4 * orders
        return View(self.store, self.used - 4 * orders, orders)


FIXED = 4 * (3 + ORDERS)
PLACES = 4 * (ORDERS + 3 * (3 * ORDERS + 1))


class Field:
    def __init__(self, shelf):
        self.value, self.turned, self.term, self.level = shelf.field(), shelf.field(), shelf.field(), shelf.planes()


def around(field, row, tile, order):
    e, beyond = field.value[row, tile, order], field.value[row, tile ^ 2, order]
    along_y = field.value[row, tile ^ 1, order] + field.turned[row, tile, order]
    along_z = beyond + pltpu.roll(beyond, 1 if tile < 2 else 7, 0)
    return e, (along_y + along_z) + (field.value[row - 1, tile, order] + field.value[row + 1, tile, order])


MOVES = (
    (1, 1, 0, 2, 6, 4, 2),
    (-1, 1, 0, 2, 6, 4, 10),
    (2, 3, 0, 1, 8, 2, 0),
    (-2, 3, 0, 1, 6, 2, 14),
    (2, 3, 1, 1, 9, 1, 1),
    (-2, 3, 1, 1, 6, 1, 14),
)
HANDED = ((1, 4, 2, 6), (1, 10, 2, 7), (3, 2, 4, 6), (3, 10, 4, 7), (3, 1, 1, 8), (3, 14, 1, 9))


def annealing_kernel(
    lab_hbm, msk_hbm, class_hbm, energy_hbm, start_hbm, end_hbm,
    cells, class_ref, energy_ref, result, in_sem, send_sem, recv_sem, out_sem, deal, gather, code, marks, fixed, store_a, store_b,
):
    tm, me = lax.axis_index("tm"), lax.axis_index("space")
    count = lax.axis_size("space")
    place = lax.rem(me, 4)

    local_copies = [
        pltpu.make_async_copy(
            src.at[:, :, pl.ds(128 * half, 128)], cells.at[k, half, pl.ds(HALO, ROWS)], in_sem.at[2 * k + half]
        )
        for k, src in enumerate((lab_hbm, msk_hbm))
        for half in (0, 1)
    ]
    table_copies = [
        pltpu.make_async_copy(class_hbm, class_ref, in_sem.at[4]),
        pltpu.make_async_copy(energy_hbm, energy_ref, in_sem.at[5]),
    ]
    for copy in local_copies + table_copies:
        copy.start()

    def partner(distance):
        crossed = jnp.where(jnp.logical_or(place + distance < 0, place + distance > 3), 1, 0)
        half = lax.rem(tm // 2 + crossed, 2)
        return half * 2 + lax.rem(tm, 2), lax.rem(me + distance + count, count)

    odd = lax.rem(tm, 2) == 1

    def greet(device):
        pl.semaphore_signal(barrier, inc=1, device_id=device, device_id_type=MESH)

    barrier = pltpu.get_barrier_semaphore()

    @pl.when(odd)
    def _():
        for distance in (1, -1):
            greet(partner(distance))

    @pl.when(tm == 3)
    def _():
        for distance in (2, -2):
            greet(partner(distance))

    @pl.when(jnp.logical_not(odd))
    def _():
        greet((tm + 1, me))

    far = [partner(distance)[0] == 3 for distance in (2, -2)]

    def halo(moves, sending, act):
        for m in moves:
            distance, least, array, arrays, first, rows, there = MOVES[m]
            target = partner(distance)
            copy = pltpu.make_async_remote_copy(
                src_ref=cells.at[pl.ds(array, arrays), :, pl.ds(first, rows)],
                dst_ref=cells.at[pl.ds(array, arrays), :, pl.ds(there, rows)],
                send_sem=send_sem.at[m],
                recv_sem=recv_sem.at[m],
                device_id=target,
                device_id_type=MESH,
            )
            receiver = target[0] if sending else tm
            wanted = jnp.logical_and(odd, receiver >= least)
            pl.when(wanted)(functools.partial(act, copy))

    def hand(copies, sending, act):
        for h in copies:
            holder, first, rows, sem = HANDED[h]
            copy = pltpu.make_async_remote_copy(
                src_ref=cells.at[:, :, pl.ds(first, rows)],
                dst_ref=cells.at[:, :, pl.ds(first, rows)],
                send_sem=send_sem.at[sem],
                recv_sem=recv_sem.at[sem],
                device_id=(holder - 1, me),
                device_id_type=MESH,
            )
            pl.when(tm == (holder if sending else holder - 1))(functools.partial(act, copy))

    start, sent, received = (lambda copy: copy.start()), (lambda copy: copy.wait_send()), (lambda copy: copy.wait_recv())

    for row in (0, EXT - 1):
        for half in (0, 1):
            cells[1, half, row] = jnp.zeros((16, 128), jnp.int32)
    for copy in local_copies:
        copy.wait()

    @pl.when(odd)
    def _():
        pl.semaphore_wait(barrier, 3 + jnp.where(far[0], 1, 0) + jnp.where(far[1], 1, 0))

    halo(range(6), True, start)

    for copy in table_copies:
        copy.wait()
    deal[...] = order_of_lanes(0)
    gather[...] = order_of_lanes(1)
    classes = jnp.broadcast_to(class_ref[...], (8, 128))
    table = jnp.full((8, 128), energy_ref[0], jnp.float32)
    for kind in range(1, 4):
        table = jnp.where(classes == kind, energy_ref[kind], table)

    shelf = Shelf(fixed)
    rate, base, weight, drive = shelf.planes(), shelf.planes(), shelf.planes(), shelf.field()
    shelf = Shelf(store_a)
    held_a, (a1, c1p, c2) = shelf.field(), [Field(shelf) for _ in range(3)]
    shelf = Shelf(store_b)
    held_b, (a1p, b2, c2p) = shelf.field(), [Field(shelf) for _ in range(3)]
    a2, b2p, b3 = a1, c1p, c2
    u0p, c1 = d3, b3p = a1p, b2

    def unpack(first, rows):
        for zt in (0, 1):
            found = None
            for half in (0, 1):
                there = (pl.ds(first, rows), pl.ds(zt, 8, stride=2))
                both = cells[0, half, *there] + 128 * cells[1, half, *there]
                part = jnp.dot(
                    both.astype(jnp.float32).reshape(rows * 8, 128).astype(jnp.bfloat16),
                    deal[pl.ds(128 * half, 128), :],
                    preferred_element_type=jnp.float32,
                )
                found = part if found is None else found + part
            found = found.astype(jnp.int32).reshape(rows, 8, 256)
            for yt in (0, 1):
                code[pl.ds(first, rows), 2 * zt + yt] = found[:, :, 128 * yt : 128 * yt + 128]

    def prepare(row):
        for tile in range(4):
            both = code[row, tile]
            label = both & 127
            rate[row, tile] = jnp.where(both > 127, 0.25 * FINE_DT, FINE_DT)
            stored = jnp.take_along_axis(table, label, axis=1, mode="promise_in_bounds")
            base[row, tile] = 1.5 * stored + 5.0
            weight[row, tile] = ROOT2 * stored + ROOT2 * 6.0
            order = both & (ORDERS - 1)
            mark = jnp.left_shift(1, 4 * order)
            marks[row, tile] = mark
            marks[row, 4 + (tile ^ 1)] = pltpu.roll(mark, TURN[1 - (tile & 1)], 1)
            for p in range(ORDERS):
                drive[row, tile, p] = jnp.where(order == p, stored, 0.0)

    def pairs(first, count, body):
        def once(k, carry):
            body(first + 2 * k)
            body(first + 2 * k + 1)
            return carry
        lax.fori_loop(0, count, once, 0)

    def level_of(name, body):
        reach = by_slice(tm, REACH[name])
        pairs(HALO - reach, jnp.where(reach < 0, 0, ROWS // 2 + reach), body)

    class Made:
        def __init__(self, field, row):
            self.field, self.row, self.total = field, row, [None] * 4

        def __call__(self, tile, p, value):
            self.field.value[self.row, tile, p] = value
            self.field.turned[self.row, tile ^ 1, p] = pltpu.roll(value, TURN[1 - (tile & 1)], 1)
            part = value * value - drive[self.row, tile, p]
            self.field.term[self.row, tile, p] = part
            self.total[tile] = part if p == 0 else self.total[tile] + part
            if p == ORDERS - 1:
                self.field.level[self.row, tile] = 1.5 * self.total[tile] + base[self.row, tile]

    def force(field, row, tile, p):
        e, beside = around(field, row, tile, p)
        return e, beside + e * (field.term[row, tile, p] - field.level[row, tile])

    def changed(field, row, tile, p, speed):
        e, push = force(field, row, tile, p)
        return e, speed * push

    even = lax.rem(lax.broadcasted_iota(jnp.int32, (8, 128), 1), 2) == 0
    spread = [lax.broadcasted_iota(jnp.int32, (8, 128), 1) // 2 + 64 * half for half in (0, 1)]

    def together(which, row, p, zt, tiles):
        for half in (0, 1):
            left, right = (jnp.take_along_axis(t, spread[half], axis=1, mode="promise_in_bounds") for t in tiles)
            result[which, half, p, row - HALO + 1, pl.ds(zt, 8, stride=2), :] = jnp.where(even, left, right) * (1.0 / ROOT2)

    def level1(row):
        new_u0p, new_c1 = Made(u0p, row), Made(c1, row)
        for tile in range(4):
            beyond = marks[row, tile ^ 2]
            beside = marks[row, tile ^ 1] + marks[row, 4 + tile] + beyond + pltpu.roll(beyond, 1 if tile < 2 else 7, 0)
            beside = beside + marks[row - 1, tile] + marks[row + 1, tile]
            order = code[row, tile] & (ORDERS - 1)
            speed = rate[row, tile]
            quick, own = ROOT2 * speed, ROOT2 - speed * weight[row, tile]
            for p in range(ORDERS):
                mine = order == p
                share = quick * (jnp.right_shift(beside, 4 * p) & 7).astype(jnp.float32)
                half = share + jnp.where(mine, own, 0.0)
                new_u0p(tile, p, half)
                new_c1(tile, p, (half + half) - jnp.where(mine, ROOT2, 0.0))

    def level2(row):
        new_a1, new_c1p, new_c2 = Made(a1, row), Made(c1p, row), Made(c2, row)
        for tile in range(4):
            speed = rate[row, tile]
            for p in range(ORDERS):
                e, change = changed(u0p, row, tile, p, speed)
                new_a1(tile, p, e + change)
            for p in range(ORDERS):
                e, change = changed(c1, row, tile, p, speed)
                half = e + change
                new_c1p(tile, p, half)
                new_c2(tile, p, half + change)
                held_a[row, tile, p] = change

    def level3(row):
        new_a1p, new_b2, new_c2p = Made(a1p, row), Made(b2, row), Made(c2p, row)
        for tile in range(4):
            speed = rate[row, tile]
            for p in range(ORDERS):
                jump = changed(c1p, row, tile, p, speed)[1] - held_a[row, tile, p]
                e, change = changed(a1, row, tile, p, speed)
                half = e + change
                new_a1p(tile, p, half)
                new_b2(tile, p, half + (change + jump))
            for p in range(ORDERS):
                e, change = changed(c2, row, tile, p, speed)
                new_c2p(tile, p, e + change)
                held_b[row, tile, p] = change

    def level4(row):
        new_a2, new_b2p, new_b3 = Made(a2, row), Made(b2p, row), Made(b3, row)
        for tile in range(4):
            speed = rate[row, tile]
            for p in range(ORDERS):
                e, change = changed(a1p, row, tile, p, speed)
                new_a2(tile, p, e + change)
            for p in range(ORDERS):
                jump = changed(c2p, row, tile, p, speed)[1] - held_b[row, tile, p]
                e, push = force(b2, row, tile, p)
                change = speed * push
                half = e + change
                new_b2p(tile, p, half)
                new_b3(tile, p, half + (change + jump))
                held_a[row, tile, p] = push

    def level5(row):
        which = jnp.where(tm == 2, 1, 0)
        new_d3, new_b3p = Made(d3, row), Made(b3p, row)
        for zt in (0, 1):
            for p in range(ORDERS):
                tiles = []
                for tile in (2 * zt, 2 * zt + 1):
                    jump = force(b2p, row, tile, p)[1] - held_a[row, tile, p]
                    e, push = force(a2, row, tile, p)
                    tiles.append(e + rate[row, tile] * (push + (push + jump)))
                    new_d3(tile, p, tiles[-1])
                together(which, row, p, zt, tiles)
        for tile in range(4):
            speed = rate[row, tile]
            for p in range(ORDERS):
                e, push = force(b3, row, tile, p)
                new_b3p(tile, p, e + speed * push)
                held_b[row, tile, p] = push

    def level6(row):
        for zt in (0, 1):
            for p in range(ORDERS):
                tiles = []
                for tile in (2 * zt, 2 * zt + 1):
                    jump = force(b3p, row, tile, p)[1] - held_b[row, tile, p]
                    e, push = force(d3, row, tile, p)
                    tiles.append(e + rate[row, tile] * (push + (push + jump)))
                together(1, row, p, zt, tiles)

    outs = (start_hbm, end_hbm)

    def sends(which):
        return [
            pltpu.make_async_copy(
                result.at[which, half, :, pl.ds(1, ROWS)],
                outs[which].at[0, :, :, :, pl.ds(128 * half, 128)],
                out_sem.at[2 * which + half],
            )
            for half in (0, 1)
        ]

    def send(ends, starts):
        for which, holder in enumerate((starts, ends)):
            @pl.when(tm == holder)
            def _():
                for copy in sends(which):
                    copy.start()

    def write(field, ends, starts):
        @pl.when(jnp.logical_or(tm == ends, tm == starts))
        def _():
            which = jnp.where(tm == ends, 1, 0)
            for zt in (0, 1):
                pieces = []
                for yt in (0, 1):
                    rest = field.value.brick(2 * zt + yt).reshape(ROWS * ORDERS * 8, 128) * (1.0 / ROOT2)
                    parts = []
                    for _ in range(3):
                        parts.append(rest.astype(jnp.bfloat16))
                        rest = rest - parts[-1].astype(jnp.float32)
                    pieces.append(parts)
                mixed = None
                for left, right in zip(*pieces):
                    moved = jnp.dot(jnp.concatenate([left, right], axis=1), gather[...], preferred_element_type=jnp.float32)
                    mixed = moved if mixed is None else mixed + moved
                mixed = mixed.reshape(ROWS, ORDERS, 8, 256)
                for row in range(ROWS):
                    for half in (0, 1):
                        result[which, half, :, row + 1, pl.ds(zt, 8, stride=2), :] = mixed[row, :, :, 128 * half : 128 * half + 128]

        send(ends, starts)

    @pl.when(tm == 0)
    def _():
        for half in (0, 1):
            for row in range(ROWS):
                order = cells[0, half, HALO + row] & (ORDERS - 1)
                for p in range(ORDERS):
                    result[0, half, p, row + 1] = jnp.where(order == p, 1.0, 0.0)

    send(-1, 0)
    unpack(HALO, ROWS)
    pairs(HALO, ROWS // 2, prepare)
    halo((0, 1), False, received)
    hand((0, 1, 2, 3), True, start)
    hand((0, 1, 2, 3), False, received)
    for first in (HALO - 4, HALO + ROWS):
        unpack(first, 4)
        pairs(first, 2, prepare)
    reach = by_slice(tm, REACH["1"])
    nearer = jnp.minimum(reach, 3)
    pairs(HALO - nearer, ROWS // 2 + nearer, level1)
    halo((2, 3, 4, 5), False, received)
    hand((4, 5), True, start)
    hand((4, 5), False, received)

    @pl.when(reach > 3)
    def _():
        for first in (0, EXT - 2):
            unpack(first, 2)
        pairs(0, 2, lambda row: prepare(jnp.where(row >= 2, row + EXT - 4, row)))
        pairs(0, 2, lambda row: level1(jnp.where(row >= 2, row + EXT - 5, row + 1)))

    level_of("2", level2)
    write(a1, 0, 1)
    level_of("3", level3)
    level_of("4", level4)
    write(a2, 1, 2)
    level_of("5", level5)
    send(2, 3)
    level_of("6", level6)
    send(3, -1)
    halo(range(6), True, sent)
    hand(range(6), True, sent)
    for which in (0, 1):
        for copy in sends(which):
            copy.wait()


def annealing(labels, particles, grain_class, class_energy):
    out = jax.ShapeDtypeStruct((1, ORDERS, ROWS, 16, 256), jnp.float32)
    arguments = [labels, particles, grain_class.reshape(1, -1), class_energy]
    return pl.pallas_call(
        annealing_kernel,
        out_shape=(out, out),
        in_specs=[pl.BlockSpec(memory_space=pltpu.HBM)] * 4,
        out_specs=[pl.BlockSpec(memory_space=pl.ANY)] * 2,
        scratch_shapes=[
            pltpu.VMEM((2, 2, EXT, 16, 128), jnp.int32),
            pltpu.VMEM((1, 128), jnp.int32),
            pltpu.SMEM((4,), jnp.float32),
            pltpu.VMEM((2, 2, ORDERS, ROWS + 2, 16, 128), jnp.float32),
            pltpu.SemaphoreType.DMA((6,)),
            pltpu.SemaphoreType.DMA((10,)),
            pltpu.SemaphoreType.DMA((10,)),
            pltpu.SemaphoreType.DMA((4,)),
            pltpu.VMEM((256, 256), jnp.bfloat16),
            pltpu.VMEM((256, 256), jnp.bfloat16),
            pltpu.VMEM((EXT, 4, 8, 128), jnp.int32),
            pltpu.VMEM((EXT, 8, 8, 128), jnp.int32),
        ]
        + [pltpu.VMEM((EXT, places, 8, 128), jnp.float32) for places in (FIXED, PLACES, PLACES)],
        compiler_params=pltpu.CompilerParams(
            collective_id=0, has_side_effects=True, vmem_limit_bytes=52 * 1024 * 1024
        ),
        name="annealing",
    )(*(pltpu.with_memory_space_constraint(a, pltpu.HBM) for a in arguments))


def solution(mesh):
    placed = (P("space", None, None), P("space", None, None), P(), P())
    return jax.shard_map(
        annealing,
        mesh=mesh,
        in_specs=placed,
        out_specs=(P("tm", None, "space", None, None), P("tm", None, "space", None, None)),
        check_vma=False,
    )
```

```python
import functools
import math

import jax
import jax.numpy as jnp
from jax import lax
from jax.experimental import pallas as pl
from jax.experimental.pallas import tpu as pltpu
from jax.sharding import PartitionSpec as P

MESH = pl.DeviceIdType.MESH
ORDERS = 8
HALO = 6
ROWS = 4
EXT = ROWS + 2 * HALO
FINE_DT = 0.06
ROOT2 = math.sqrt(2.0)

REACH = {
    "1": (1, 3, 4, 5),
    "2": (0, 2, 3, 4),
    "3": (-1, 1, 2, 3),
    "4": (-1, 0, 1, 2),
    "5": (-1, -1, 0, 1),
    "6": (-1, -1, -1, 0),
}


def by_slice(tm, values):
    result = jnp.int32(values[0])
    for index in range(1, len(values)):
        result = jnp.where(tm >= index, jnp.int32(values[index]), result)
    return result


TURN = (1, 127)


def order_of_lanes(across):
    y = lax.broadcasted_iota(jnp.int32, (256, 256), across)
    place = lax.broadcasted_iota(jnp.int32, (256, 256), 1 - across)
    return jnp.where(y == 2 * (place & 127) + (place >> 7), 1.0, 0.0).astype(jnp.bfloat16)


class View:
    def __init__(self, store, first, orders):
        self.store, self.first, self.orders = store, first, orders

    def at(self, index):
        return (index[0], self.first + index[1] * self.orders + (index[2] if self.orders > 1 else 0))

    def __getitem__(self, index):
        return self.store[self.at(index)]

    def __setitem__(self, index, tile):
        self.store[self.at(index)] = tile

    def brick(self, tile):
        return self.store[pl.ds(HALO, ROWS), pl.ds(self.first + tile * self.orders, self.orders)]


class Shelf:
    def __init__(self, store):
        self.store, self.used = store, 0

    def planes(self):
        return self.view(1)

    def field(self):
        return self.view(ORDERS)

    def view(self, orders):
        self.used += 4 * orders
        return View(self.store, self.used - 4 * orders, orders)


FIXED = 4 * (3 + ORDERS)
PLACES = 4 * (ORDERS + 3 * (3 * ORDERS + 1))


class Field:
    def __init__(self, shelf):
        self.value, self.turned, self.term, self.level = shelf.field(), shelf.field(), shelf.field(), shelf.planes()


def around(field, row, tile, order):
    e, beyond = field.value[row, tile, order], field.value[row, tile ^ 2, order]
    along_y = field.value[row, tile ^ 1, order] + field.turned[row, tile, order]
    along_z = beyond + pltpu.roll(beyond, 1 if tile < 2 else 7, 0)
    return e, (along_y + along_z) + (field.value[row - 1, tile, order] + field.value[row + 1, tile, order])


MOVES = (
    (1, 1, 0, 2, 6, 4, 2),
    (-1, 1, 0, 2, 6, 4, 10),
    (2, 3, 0, 1, 8, 2, 0),
    (-2, 3, 0, 1, 6, 2, 14),
    (2, 3, 1, 1, 9, 1, 1),
    (-2, 3, 1, 1, 6, 1, 14),
)
HANDED = ((1, 4, 2, 6), (1, 10, 2, 7), (3, 2, 4, 6), (3, 10, 4, 7), (3, 1, 1, 8), (3, 14, 1, 9))


SIDES = (((0,), (2, 4), (0, 2), (4,)), ((1,), (3, 5), (1, 3), (5,)))


def annealing_kernel(
    lab_hbm, msk_hbm, class_hbm, energy_hbm, start_hbm, end_hbm,
    cells, class_ref, energy_ref, result, in_sem, send_sem, recv_sem, out_sem, deal, gather, code, marks, fixed, store_a, store_b,
):
    tm, me = lax.axis_index("tm"), lax.axis_index("space")
    count = lax.axis_size("space")
    place = lax.rem(me, 4)

    local_copies = [
        pltpu.make_async_copy(
            src.at[:, :, pl.ds(128 * half, 128)], cells.at[k, half, pl.ds(HALO, ROWS)], in_sem.at[2 * k + half]
        )
        for k, src in enumerate((lab_hbm, msk_hbm))
        for half in (0, 1)
    ]
    table_copies = [
        pltpu.make_async_copy(class_hbm, class_ref, in_sem.at[4]),
        pltpu.make_async_copy(energy_hbm, energy_ref, in_sem.at[5]),
    ]
    for copy in local_copies + table_copies:
        copy.start()

    def partner(distance):
        crossed = jnp.where(jnp.logical_or(place + distance < 0, place + distance > 3), 1, 0)
        half = lax.rem(tm // 2 + crossed, 2)
        return half * 2 + lax.rem(tm, 2), lax.rem(me + distance + count, count)

    odd = lax.rem(tm, 2) == 1

    def greet(device):
        pl.semaphore_signal(barrier, inc=1, device_id=device, device_id_type=MESH)

    barrier = pltpu.get_barrier_semaphore()

    @pl.when(odd)
    def _():
        for distance in (1, -1):
            greet(partner(distance))

    @pl.when(tm == 3)
    def _():
        for distance in (2, -2):
            greet(partner(distance))

    @pl.when(jnp.logical_not(odd))
    def _():
        greet((tm + 1, me))

    far = [partner(distance)[0] == 3 for distance in (2, -2)]

    def halo(moves, sending, act):
        for m in moves:
            distance, least, array, arrays, first, rows, there = MOVES[m]
            target = partner(distance)
            copy = pltpu.make_async_remote_copy(
                src_ref=cells.at[pl.ds(array, arrays), :, pl.ds(first, rows)],
                dst_ref=cells.at[pl.ds(array, arrays), :, pl.ds(there, rows)],
                send_sem=send_sem.at[m],
                recv_sem=recv_sem.at[m],
                device_id=target,
                device_id_type=MESH,
            )
            receiver = target[0] if sending else tm
            wanted = jnp.logical_and(odd, receiver >= least)
            pl.when(wanted)(functools.partial(act, copy))

    def hand(copies, sending, act):
        for h in copies:
            holder, first, rows, sem = HANDED[h]
            copy = pltpu.make_async_remote_copy(
                src_ref=cells.at[:, :, pl.ds(first, rows)],
                dst_ref=cells.at[:, :, pl.ds(first, rows)],
                send_sem=send_sem.at[sem],
                recv_sem=recv_sem.at[sem],
                device_id=(holder - 1, me),
                device_id_type=MESH,
            )
            pl.when(tm == (holder if sending else holder - 1))(functools.partial(act, copy))

    start, sent, received = (lambda copy: copy.start()), (lambda copy: copy.wait_send()), (lambda copy: copy.wait_recv())

    for row in (0, EXT - 1):
        for half in (0, 1):
            cells[1, half, row] = jnp.zeros((16, 128), jnp.int32)
    for copy in local_copies:
        copy.wait()

    @pl.when(odd)
    def _():
        pl.semaphore_wait(barrier, 3 + jnp.where(far[0], 1, 0) + jnp.where(far[1], 1, 0))

    halo(range(6), True, start)

    for copy in table_copies:
        copy.wait()
    deal[...] = order_of_lanes(0)
    gather[...] = order_of_lanes(1)
    classes = jnp.broadcast_to(class_ref[...], (8, 128))
    table = jnp.full((8, 128), energy_ref[0], jnp.float32)
    for kind in range(1, 4):
        table = jnp.where(classes == kind, energy_ref[kind], table)

    shelf = Shelf(fixed)
    rate, base, weight, drive = shelf.planes(), shelf.planes(), shelf.planes(), shelf.field()
    shelf = Shelf(store_a)
    held_a, (a1, c1p, c2) = shelf.field(), [Field(shelf) for _ in range(3)]
    shelf = Shelf(store_b)
    held_b, (a1p, b2, c2p) = shelf.field(), [Field(shelf) for _ in range(3)]
    a2, b2p, b3 = a1, c1p, c2
    e4 = a1
    u0p, c1 = d3, b3p = a1p, b2

    def unpack(first, rows):
        for zt in (0, 1):
            found = None
            for half in (0, 1):
                there = (pl.ds(first, rows), pl.ds(zt, 8, stride=2))
                both = cells[0, half, *there] + 128 * cells[1, half, *there]
                part = jnp.dot(
                    both.astype(jnp.float32).reshape(rows * 8, 128).astype(jnp.bfloat16),
                    deal[pl.ds(128 * half, 128), :],
                    preferred_element_type=jnp.float32,
                )
                found = part if found is None else found + part
            found = found.astype(jnp.int32).reshape(rows, 8, 256)
            for yt in (0, 1):
                code[pl.ds(first, rows), 2 * zt + yt] = found[:, :, 128 * yt : 128 * yt + 128]

    def prepare(row):
        for tile in range(4):
            both = code[row, tile]
            label = both & 127
            rate[row, tile] = jnp.where(both > 127, 0.25 * FINE_DT, FINE_DT)
            stored = jnp.take_along_axis(table, label, axis=1, mode="promise_in_bounds")
            base[row, tile] = 1.5 * stored + 5.0
            weight[row, tile] = ROOT2 * stored + ROOT2 * 6.0
            order = both & (ORDERS - 1)
            mark = jnp.left_shift(1, 4 * order)
            marks[row, tile] = mark
            marks[row, 4 + (tile ^ 1)] = pltpu.roll(mark, TURN[1 - (tile & 1)], 1)
            for p in range(ORDERS):
                drive[row, tile, p] = jnp.where(order == p, stored, 0.0)

    def pairs(first, count, body):
        def once(k, carry):
            body(first + 2 * k)
            body(first + 2 * k + 1)
            return carry
        lax.fori_loop(0, count, once, 0)

    def level_of(name, body):
        reach = by_slice(tm, REACH[name])
        pairs(HALO - reach, jnp.where(reach < 0, 0, ROWS // 2 + reach), body)

    class Made:
        def __init__(self, field, row):
            self.field, self.row, self.total = field, row, [None] * 4

        def __call__(self, tile, p, value):
            self.field.value[self.row, tile, p] = value
            self.field.turned[self.row, tile ^ 1, p] = pltpu.roll(value, TURN[1 - (tile & 1)], 1)
            part = value * value - drive[self.row, tile, p]
            self.field.term[self.row, tile, p] = part
            self.total[tile] = part if p == 0 else self.total[tile] + part
            if p == ORDERS - 1:
                self.field.level[self.row, tile] = 1.5 * self.total[tile] + base[self.row, tile]

    def force(field, row, tile, p):
        e, beside = around(field, row, tile, p)
        return e, beside + e * (field.term[row, tile, p] - field.level[row, tile])

    def changed(field, row, tile, p, speed):
        e, push = force(field, row, tile, p)
        return e, speed * push

    def level1(row):
        new_u0p, new_c1 = Made(u0p, row), Made(c1, row)
        for tile in range(4):
            beside = counts(row, tile)
            order = code[row, tile] & (ORDERS - 1)
            speed = rate[row, tile]
            quick, own = ROOT2 * speed, ROOT2 - speed * weight[row, tile]
            for p in range(ORDERS):
                mine = order == p
                share = quick * (jnp.right_shift(beside, 4 * p) & 7).astype(jnp.float32)
                half = share + jnp.where(mine, own, 0.0)
                new_u0p(tile, p, half)
                new_c1(tile, p, (half + half) - jnp.where(mine, ROOT2, 0.0))

    def level2(row):
        new_a1, new_c1p, new_c2 = Made(a1, row), Made(c1p, row), Made(c2, row)
        for tile in range(4):
            speed = rate[row, tile]
            for p in range(ORDERS):
                e, change = changed(u0p, row, tile, p, speed)
                new_a1(tile, p, e + change)
            for p in range(ORDERS):
                e, change = changed(c1, row, tile, p, speed)
                half = e + change
                new_c1p(tile, p, half)
                new_c2(tile, p, half + change)
                held_a[row, tile, p] = change

    def level3(row):
        new_a1p, new_b2, new_c2p = Made(a1p, row), Made(b2, row), Made(c2p, row)
        for tile in range(4):
            speed = rate[row, tile]
            for p in range(ORDERS):
                jump = changed(c1p, row, tile, p, speed)[1] - held_a[row, tile, p]
                e, change = changed(a1, row, tile, p, speed)
                half = e + change
                new_a1p(tile, p, half)
                new_b2(tile, p, half + (change + jump))
            for p in range(ORDERS):
                e, change = changed(c2, row, tile, p, speed)
                new_c2p(tile, p, e + change)
                held_b[row, tile, p] = change

    def level4(row):
        new_a2, new_b2p, new_b3 = Made(a2, row), Made(b2p, row), Made(b3, row)
        for tile in range(4):
            speed = rate[row, tile]
            for p in range(ORDERS):
                e, change = changed(a1p, row, tile, p, speed)
                new_a2(tile, p, e + change)
            for p in range(ORDERS):
                jump = changed(c2p, row, tile, p, speed)[1] - held_b[row, tile, p]
                e, push = force(b2, row, tile, p)
                change = speed * push
                half = e + change
                new_b2p(tile, p, half)
                new_b3(tile, p, half + (change + jump))
                held_a[row, tile, p] = push

    def level5(row):
        new_d3, new_b3p = Made(d3, row), Made(b3p, row)
        for tile in range(4):
            speed = rate[row, tile]
            for p in range(ORDERS):
                jump = force(b2p, row, tile, p)[1] - held_a[row, tile, p]
                e, push = force(a2, row, tile, p)
                new_d3(tile, p, e + speed * (push + (push + jump)))
            for p in range(ORDERS):
                e, push = force(b3, row, tile, p)
                new_b3p(tile, p, e + speed * push)
                held_b[row, tile, p] = push

    def level6(row):
        for tile in range(4):
            speed = rate[row, tile]
            for p in range(ORDERS):
                jump = force(b3p, row, tile, p)[1] - held_b[row, tile, p]
                e, push = force(d3, row, tile, p)
                e4.value[row, tile, p] = e + speed * (push + (push + jump))

    def counts(row, tile):
        beyond = marks[row, tile ^ 2]
        beside = marks[row, tile ^ 1] + marks[row, 4 + tile] + beyond + pltpu.roll(beyond, 1 if tile < 2 else 7, 0)
        return beside + marks[row - 1, tile] + marks[row + 1, tile]

    def short1(row):
        new_u0p = Made(u0p, row)
        for tile in range(4):
            beside, order, speed = counts(row, tile), code[row, tile] & (ORDERS - 1), rate[row, tile]
            quick, own = ROOT2 * speed, ROOT2 - speed * weight[row, tile]
            for p in range(ORDERS):
                share = quick * (jnp.right_shift(beside, 4 * p) & 7).astype(jnp.float32)
                new_u0p(tile, p, share + jnp.where(order == p, own, 0.0))

    def short(field, made):
        def body(row):
            new = Made(made, row)
            for tile in range(4):
                speed = rate[row, tile]
                for p in range(ORDERS):
                    e, change = changed(field, row, tile, p, speed)
                    new(tile, p, e + change)
        return body

    def short4(row):
        for tile in range(4):
            speed = rate[row, tile]
            for p in range(ORDERS):
                e, change = changed(a1p, row, tile, p, speed)
                a2.value[row, tile, p] = e + change

    outs = (start_hbm, end_hbm)

    def sends(which):
        return [
            pltpu.make_async_copy(
                result.at[which, half, :, pl.ds(1, ROWS)],
                outs[which].at[0, :, :, :, pl.ds(128 * half, 128)],
                out_sem.at[2 * which + half],
            )
            for half in (0, 1)
        ]

    def send(ends, starts):
        for which, holder in enumerate((starts, ends)):
            @pl.when(tm == holder)
            def _():
                for copy in sends(which):
                    copy.start()

    def write(field, ends, starts):
        @pl.when(jnp.logical_or(tm == ends, tm == starts))
        def _():
            which = jnp.where(tm == ends, 1, 0)
            for zt in (0, 1):
                pieces = []
                for yt in (0, 1):
                    rest = field.value.brick(2 * zt + yt).reshape(ROWS * ORDERS * 8, 128)
                    parts = []
                    for _ in range(2):
                        parts.append(rest.astype(jnp.bfloat16))
                        rest = rest - parts[-1].astype(jnp.float32)
                    pieces.append(parts)
                mixed = None
                for left, right in zip(*pieces):
                    moved = jnp.dot(jnp.concatenate([left, right], axis=1), gather[...], preferred_element_type=jnp.float32)
                    mixed = moved if mixed is None else mixed + moved
                mixed = mixed.reshape(ROWS, ORDERS, 8, 256)
                for row in range(ROWS):
                    for half in (0, 1):
                        result[which, half, :, row + 1, pl.ds(zt, 8, stride=2), :] = mixed[row, :, :, 128 * half : 128 * half + 128]

        send(ends, starts)

    @pl.when(tm == 0)
    def _():
        for half in (0, 1):
            for row in range(ROWS):
                order = cells[0, half, HALO + row] & (ORDERS - 1)
                for p in range(ORDERS):
                    result[0, half, p, row + 1] = jnp.where(order == p, ROOT2, 0.0)

    send(-1, 0)
    unpack(HALO, ROWS)
    pairs(HALO, ROWS // 2, prepare)

    low_late = jnp.logical_or(place < 2, me == 2)

    def split(level, phase, lo, hi):
        reach = by_slice(tm, REACH[level])
        total = jnp.where(reach < 0, 0, ROWS // 2 + reach)
        depth = int(level)
        low = jnp.minimum((depth + reach + 1) // 2, total)
        high = total - jnp.maximum((ROWS - depth + reach) // 2, 0)
        late = jnp.where(low_late, low, high)
        late = jnp.clip(late, 0, total)
        number = jnp.where(phase == 0, total - late, late)
        at_low = jnp.logical_xor(low_late, phase == 0)
        first = HALO - reach + jnp.where(at_low, 0, 2 * (total - number))
        return first, jnp.where(jnp.logical_and(tm >= lo, tm <= hi), number, 0)

    def phases(phase, carry):
        at_low = jnp.logical_xor(low_late, phase == 0)
        for side, (halos, far_halos, hands, far_hands) in enumerate(SIDES):
            @pl.when(at_low if side == 0 else jnp.logical_not(at_low))
            def _():
                halo(halos, False, received)
                hand(hands, True, start)
                hand(hands, False, received)
        first = jnp.where(at_low, HALO - 4, HALO + ROWS)
        unpack(first, 4)
        pairs(first, 2, prepare)
        for side, (halos, far_halos, hands, far_hands) in enumerate(SIDES):
            @pl.when(at_low if side == 0 else jnp.logical_not(at_low))
            def _():
                halo(far_halos, False, received)
                hand(far_hands, True, start)
                hand(far_hands, False, received)

        @pl.when(tm >= 2)
        def _():
            outer = jnp.where(at_low, 0, EXT - 2)
            unpack(outer, 2)
            pairs(outer, 1, prepare)

        pairs(*split("1", phase, 2, 3), level1)
        pairs(*split("1", phase, 0, 1), short1)
        pairs(*split("2", phase, 2, 3), level2)
        pairs(*split("2", phase, 0, 1), short(u0p, a1))

        @pl.when(phase == 1)
        def _():
            write(a1, 0, 1)

        pairs(*split("3", phase, 2, 3), level3)
        pairs(*split("3", phase, 0, 1), short(a1, a1p))
        pairs(*split("4", phase, 2, 3), level4)
        pairs(*split("4", phase, 0, 1), short4)
        return carry

    lax.fori_loop(0, 2, phases, 0)
    write(a2, 1, 2)
    level_of("5", level5)
    write(d3, 2, 3)
    level_of("6", level6)
    write(e4, 3, -1)
    halo(range(6), True, sent)
    hand(range(6), True, sent)
    for which in (0, 1):
        for copy in sends(which):
            copy.wait()


def annealing(labels, particles, grain_class, class_energy):
    out = jax.ShapeDtypeStruct((1, ORDERS, ROWS, 16, 256), jnp.float32)
    arguments = [labels, particles, grain_class.reshape(1, -1), class_energy]
    made = pl.pallas_call(
        annealing_kernel,
        out_shape=(out, out),
        in_specs=[pl.BlockSpec(memory_space=pltpu.HBM)] * 4,
        out_specs=[pl.BlockSpec(memory_space=pl.ANY)] * 2,
        scratch_shapes=[
            pltpu.VMEM((2, 2, EXT, 16, 128), jnp.int32),
            pltpu.VMEM((1, 128), jnp.int32),
            pltpu.SMEM((4,), jnp.float32),
            pltpu.VMEM((2, 2, ORDERS, ROWS + 2, 16, 128), jnp.float32),
            pltpu.SemaphoreType.DMA((6,)),
            pltpu.SemaphoreType.DMA((10,)),
            pltpu.SemaphoreType.DMA((10,)),
            pltpu.SemaphoreType.DMA((4,)),
            pltpu.VMEM((256, 256), jnp.bfloat16),
            pltpu.VMEM((256, 256), jnp.bfloat16),
            pltpu.VMEM((EXT, 4, 8, 128), jnp.int32),
            pltpu.VMEM((EXT, 8, 8, 128), jnp.int32),
        ]
        + [pltpu.VMEM((EXT, places, 8, 128), jnp.float32) for places in (FIXED, PLACES, PLACES)],
        compiler_params=pltpu.CompilerParams(
            collective_id=0, has_side_effects=True, vmem_limit_bytes=52 * 1024 * 1024
        ),
        name="annealing",
    )(*(pltpu.with_memory_space_constraint(a, pltpu.HBM) for a in arguments))
    return tuple(part * (1.0 / ROOT2) for part in made)


def solution(mesh):
    placed = (P("space", None, None), P("space", None, None), P(), P())
    return jax.shard_map(
        annealing,
        mesh=mesh,
        in_specs=placed,
        out_specs=(P("tm", None, "space", None, None), P("tm", None, "space", None, None)),
        check_vma=False,
    )
```

```python
import functools
import math

import jax
import jax.numpy as jnp
from jax import lax
from jax.experimental import pallas as pl
from jax.experimental.pallas import tpu as pltpu
from jax.sharding import PartitionSpec as P

MESH = pl.DeviceIdType.MESH
ORDERS = 8
HALO = 6
ROWS = 4
EXT = ROWS + 2 * HALO
FINE_DT = 0.06
ROOT2 = math.sqrt(2.0)

REACH = {
    "1": (1, 3, 4, 5),
    "2": (0, 2, 3, 4),
    "3": (-1, 1, 2, 3),
    "4": (-1, 0, 1, 2),
    "5": (-1, -1, 0, 1),
    "6": (-1, -1, -1, 0),
}


def by_slice(tm, values):
    result = jnp.int32(values[0])
    for index in range(1, len(values)):
        result = jnp.where(tm >= index, jnp.int32(values[index]), result)
    return result


TURN = (1, 127)


def order_of_lanes(across):
    y = lax.broadcasted_iota(jnp.int32, (256, 256), across)
    place = lax.broadcasted_iota(jnp.int32, (256, 256), 1 - across)
    return jnp.where(y == 2 * (place & 127) + (place >> 7), 1.0, 0.0).astype(jnp.bfloat16)


class View:
    def __init__(self, store, first, orders):
        self.store, self.first, self.orders = store, first, orders

    def at(self, index):
        return (index[0], self.first + index[1] * self.orders + (index[2] if self.orders > 1 else 0))

    def __getitem__(self, index):
        return self.store[self.at(index)]

    def __setitem__(self, index, tile):
        self.store[self.at(index)] = tile

    def brick(self, tile):
        return self.store[pl.ds(HALO, ROWS), pl.ds(self.first + tile * self.orders, self.orders)]


class Shelf:
    def __init__(self, store):
        self.store, self.used = store, 0

    def planes(self):
        return self.view(1)

    def field(self):
        return self.view(ORDERS)

    def view(self, orders):
        self.used += 4 * orders
        return View(self.store, self.used - 4 * orders, orders)


FIXED = 4 * (3 + ORDERS)
PLACES = 4 * (ORDERS + 3 * (3 * ORDERS + 1))


class Field:
    def __init__(self, shelf):
        self.value, self.turned, self.term, self.level = shelf.field(), shelf.field(), shelf.field(), shelf.planes()


def around(field, row, tile, order):
    e, beyond = field.value[row, tile, order], field.value[row, tile ^ 2, order]
    along_y = field.value[row, tile ^ 1, order] + field.turned[row, tile, order]
    along_z = beyond + pltpu.roll(beyond, 1 if tile < 2 else 7, 0)
    return e, (along_y + along_z) + (field.value[row - 1, tile, order] + field.value[row + 1, tile, order])


MOVES = (
    (1, 1, 0, 2, 6, 4, 2),
    (-1, 1, 0, 2, 6, 4, 10),
    (2, 3, 0, 1, 8, 2, 0),
    (-2, 3, 0, 1, 6, 2, 14),
    (2, 3, 1, 1, 9, 1, 1),
    (-2, 3, 1, 1, 6, 1, 14),
)
HANDED = ((1, 4, 2, 6), (1, 10, 2, 7), (3, 2, 4, 6), (3, 10, 4, 7), (3, 1, 1, 8), (3, 14, 1, 9))


SIDES = (((0,), (2, 4), (0, 2), (4,)), ((1,), (3, 5), (1, 3), (5,)))


def annealing_kernel(
    lab_hbm, msk_hbm, class_hbm, energy_hbm, start_hbm, end_hbm,
    cells, class_ref, energy_ref, result, in_sem, send_sem, recv_sem, out_sem, deal, gather, code, marks, fixed, store_a, store_b,
):
    tm, me = lax.axis_index("tm"), lax.axis_index("space")
    count = lax.axis_size("space")
    place = lax.rem(me, 4)

    local_copies = [
        pltpu.make_async_copy(
            src.at[:, :, pl.ds(128 * half, 128)], cells.at[k, half, pl.ds(HALO, ROWS)], in_sem.at[2 * k + half]
        )
        for k, src in enumerate((lab_hbm, msk_hbm))
        for half in (0, 1)
    ]
    table_copies = [
        pltpu.make_async_copy(class_hbm, class_ref, in_sem.at[4]),
        pltpu.make_async_copy(energy_hbm, energy_ref, in_sem.at[5]),
    ]
    for copy in local_copies + table_copies:
        copy.start()

    odd = lax.rem(tm, 2) == 1

    def away(distance, holder):
        return holder, lax.rem(me + distance + count, count)

    def crosses(distance):
        return jnp.logical_or(place + distance < 0, place + distance > 3)

    def across(distance):
        sends = jnp.logical_and(tm == 1, crosses(distance))
        return jnp.logical_and(sends, place != 1) if distance == -2 else sends

    def greet(device):
        pl.semaphore_signal(barrier, inc=1, device_id=device, device_id_type=MESH)

    barrier = pltpu.get_barrier_semaphore()
    targets = 1
    for distance in (1, -1, 2, -2):
        one = abs(distance) == 1
        greets = odd if one else tm == 3
        if distance == 2:
            greets = jnp.logical_and(greets, place != 3)
        pl.when(greets)(
            functools.partial(greet, away(distance, jnp.where(crosses(distance), 1, tm)))
        )
        straight = jnp.where(crosses(distance), tm == 1, tm >= (1 if one else 3))
        if not one:
            straight = jnp.logical_and(straight, tm == 3)
        targets = targets + jnp.where(straight, 1, 0) + jnp.where(across(distance), 1, 0)

    @pl.when(jnp.logical_not(odd))
    def _():
        greet((tm + 1, me))

    def moved(m, over):
        distance, _, array, arrays, first, rows, there = MOVES[m]
        return pltpu.make_async_remote_copy(
            src_ref=cells.at[pl.ds(array, arrays), :, pl.ds(first, rows)],
            dst_ref=cells.at[pl.ds(array, arrays), :, pl.ds(there, rows)],
            send_sem=send_sem.at[10 * over + m],
            recv_sem=recv_sem.at[m],
            device_id=away(distance, 3 if over else tm),
            device_id_type=MESH,
        )

    def halo(act):
        for m, (distance, least, *_) in enumerate(MOVES):
            inside = jnp.logical_or(tm == 1, jnp.logical_not(crosses(distance)))
            wanted = jnp.logical_and(jnp.logical_and(odd, tm >= least), inside)
            pl.when(wanted)(functools.partial(act, moved(m, 0)))
            pl.when(across(distance))(functools.partial(act, moved(m, 1)))

    def relay(act):
        for m in (3, 5):
            _, _, array, arrays, first, rows, there = MOVES[m]
            copy = pltpu.make_async_remote_copy(
                src_ref=cells.at[pl.ds(array, arrays), :, pl.ds(first + ROWS, rows)],
                dst_ref=cells.at[pl.ds(array, arrays), :, pl.ds(there, rows)],
                send_sem=send_sem.at[13 + m],
                recv_sem=recv_sem.at[m],
                device_id=away(-1, 3),
                device_id_type=MESH,
            )
            pl.when(jnp.logical_and(tm == 1, place == 0))(functools.partial(act, copy))

    def halo_received(moves):
        for m in moves:
            pl.when(jnp.logical_and(odd, tm >= MOVES[m][1]))(moved(m, 0).wait_recv)

    def hand(copies, sending, act):
        for h in copies:
            holder, first, rows, sem = HANDED[h]
            copy = pltpu.make_async_remote_copy(
                src_ref=cells.at[:, :, pl.ds(first, rows)],
                dst_ref=cells.at[:, :, pl.ds(first, rows)],
                send_sem=send_sem.at[sem],
                recv_sem=recv_sem.at[sem],
                device_id=(holder - 1, me),
                device_id_type=MESH,
            )
            pl.when(tm == (holder if sending else holder - 1))(functools.partial(act, copy))

    start, sent, received = (lambda copy: copy.start()), (lambda copy: copy.wait_send()), (lambda copy: copy.wait_recv())

    for row in (0, EXT - 1):
        for half in (0, 1):
            cells[1, half, row] = jnp.zeros((16, 128), jnp.int32)
    for copy in local_copies:
        copy.wait()

    @pl.when(odd)
    def _():
        pl.semaphore_wait(barrier, targets)

    halo(start)

    for copy in table_copies:
        copy.wait()
    deal[...] = order_of_lanes(0)
    gather[...] = order_of_lanes(1)
    classes = jnp.broadcast_to(class_ref[...], (8, 128))
    table = jnp.full((8, 128), energy_ref[0], jnp.float32)
    for kind in range(1, 4):
        table = jnp.where(classes == kind, energy_ref[kind], table)

    shelf = Shelf(fixed)
    rate, base, weight, drive = shelf.planes(), shelf.planes(), shelf.planes(), shelf.field()
    shelf = Shelf(store_a)
    held_a, (a1, c1p, c2) = shelf.field(), [Field(shelf) for _ in range(3)]
    shelf = Shelf(store_b)
    held_b, (a1p, b2, c2p) = shelf.field(), [Field(shelf) for _ in range(3)]
    a2, b2p, b3 = a1, c1p, c2
    e4 = a1
    u0p, c1 = d3, b3p = a1p, b2

    def unpack(first, rows):
        for zt in (0, 1):
            found = None
            for half in (0, 1):
                there = (pl.ds(first, rows), pl.ds(zt, 8, stride=2))
                both = cells[0, half, *there] + 128 * cells[1, half, *there]
                part = jnp.dot(
                    both.astype(jnp.float32).reshape(rows * 8, 128).astype(jnp.bfloat16),
                    deal[pl.ds(128 * half, 128), :],
                    preferred_element_type=jnp.float32,
                )
                found = part if found is None else found + part
            found = found.astype(jnp.int32).reshape(rows, 8, 256)
            for yt in (0, 1):
                code[pl.ds(first, rows), 2 * zt + yt] = found[:, :, 128 * yt : 128 * yt + 128]

    def prepare(row):
        for tile in range(4):
            both = code[row, tile]
            label = both & 127
            rate[row, tile] = jnp.where(both > 127, 0.25 * FINE_DT, FINE_DT)
            stored = jnp.take_along_axis(table, label, axis=1, mode="promise_in_bounds")
            base[row, tile] = 1.5 * stored + 5.0
            weight[row, tile] = ROOT2 * stored + ROOT2 * 6.0
            order = both & (ORDERS - 1)
            mark = jnp.left_shift(1, 4 * order)
            marks[row, tile] = mark
            marks[row, 4 + (tile ^ 1)] = pltpu.roll(mark, TURN[1 - (tile & 1)], 1)
            for p in range(ORDERS):
                drive[row, tile, p] = jnp.where(order == p, stored, 0.0)

    def pairs(first, count, body):
        def once(k, carry):
            body(first + 2 * k)
            body(first + 2 * k + 1)
            return carry
        lax.fori_loop(0, count, once, 0)

    def level_of(name, body):
        reach = by_slice(tm, REACH[name])
        pairs(HALO - reach, jnp.where(reach < 0, 0, ROWS // 2 + reach), body)

    class Made:
        def __init__(self, field, row):
            self.field, self.row, self.total = field, row, [None] * 4

        def __call__(self, tile, p, value):
            self.field.value[self.row, tile, p] = value
            self.field.turned[self.row, tile ^ 1, p] = pltpu.roll(value, TURN[1 - (tile & 1)], 1)
            part = value * value - drive[self.row, tile, p]
            self.field.term[self.row, tile, p] = part
            self.total[tile] = part if p == 0 else self.total[tile] + part
            if p == ORDERS - 1:
                self.field.level[self.row, tile] = 1.5 * self.total[tile] + base[self.row, tile]

    def force(field, row, tile, p):
        e, beside = around(field, row, tile, p)
        return e, beside + e * (field.term[row, tile, p] - field.level[row, tile])

    def changed(field, row, tile, p, speed):
        e, push = force(field, row, tile, p)
        return e, speed * push

    def level1(row):
        new_u0p, new_c1 = Made(u0p, row), Made(c1, row)
        for tile in range(4):
            beside = counts(row, tile)
            order = code[row, tile] & (ORDERS - 1)
            speed = rate[row, tile]
            quick, own = ROOT2 * speed, ROOT2 - speed * weight[row, tile]
            for p in range(ORDERS):
                mine = order == p
                share = quick * (jnp.right_shift(beside, 4 * p) & 7).astype(jnp.float32)
                half = share + jnp.where(mine, own, 0.0)
                new_u0p(tile, p, half)
                new_c1(tile, p, (half + half) - jnp.where(mine, ROOT2, 0.0))

    def level2(row):
        new_a1, new_c1p, new_c2 = Made(a1, row), Made(c1p, row), Made(c2, row)
        for tile in range(4):
            speed = rate[row, tile]
            for p in range(ORDERS):
                e, change = changed(u0p, row, tile, p, speed)
                new_a1(tile, p, e + change)
            for p in range(ORDERS):
                e, change = changed(c1, row, tile, p, speed)
                half = e + change
                new_c1p(tile, p, half)
                new_c2(tile, p, half + change)
                held_a[row, tile, p] = change

    def level3(row):
        new_a1p, new_b2, new_c2p = Made(a1p, row), Made(b2, row), Made(c2p, row)
        for tile in range(4):
            speed = rate[row, tile]
            for p in range(ORDERS):
                jump = changed(c1p, row, tile, p, speed)[1] - held_a[row, tile, p]
                e, change = changed(a1, row, tile, p, speed)
                half = e + change
                new_a1p(tile, p, half)
                new_b2(tile, p, half + (change + jump))
            for p in range(ORDERS):
                e, change = changed(c2, row, tile, p, speed)
                new_c2p(tile, p, e + change)
                held_b[row, tile, p] = change

    def level4(row):
        new_a2, new_b2p, new_b3 = Made(a2, row), Made(b2p, row), Made(b3, row)
        for tile in range(4):
            speed = rate[row, tile]
            for p in range(ORDERS):
                e, change = changed(a1p, row, tile, p, speed)
                new_a2(tile, p, e + change)
            for p in range(ORDERS):
                jump = changed(c2p, row, tile, p, speed)[1] - held_b[row, tile, p]
                e, push = force(b2, row, tile, p)
                change = speed * push
                half = e + change
                new_b2p(tile, p, half)
                new_b3(tile, p, half + (change + jump))
                held_a[row, tile, p] = push

    def level5(row):
        new_d3, new_b3p = Made(d3, row), Made(b3p, row)
        for tile in range(4):
            speed = rate[row, tile]
            for p in range(ORDERS):
                jump = force(b2p, row, tile, p)[1] - held_a[row, tile, p]
                e, push = force(a2, row, tile, p)
                new_d3(tile, p, e + speed * (push + (push + jump)))
            for p in range(ORDERS):
                e, push = force(b3, row, tile, p)
                new_b3p(tile, p, e + speed * push)
                held_b[row, tile, p] = push

    def level6(row):
        for tile in range(4):
            speed = rate[row, tile]
            for p in range(ORDERS):
                jump = force(b3p, row, tile, p)[1] - held_b[row, tile, p]
                e, push = force(d3, row, tile, p)
                e4.value[row, tile, p] = e + speed * (push + (push + jump))

    def counts(row, tile):
        beyond = marks[row, tile ^ 2]
        beside = marks[row, tile ^ 1] + marks[row, 4 + tile] + beyond + pltpu.roll(beyond, 1 if tile < 2 else 7, 0)
        return beside + marks[row - 1, tile] + marks[row + 1, tile]

    def short1(row):
        new_u0p = Made(u0p, row)
        for tile in range(4):
            beside, order, speed = counts(row, tile), code[row, tile] & (ORDERS - 1), rate[row, tile]
            quick, own = ROOT2 * speed, ROOT2 - speed * weight[row, tile]
            for p in range(ORDERS):
                share = quick * (jnp.right_shift(beside, 4 * p) & 7).astype(jnp.float32)
                new_u0p(tile, p, share + jnp.where(order == p, own, 0.0))

    def short(field, made):
        def body(row):
            new = Made(made, row)
            for tile in range(4):
                speed = rate[row, tile]
                for p in range(ORDERS):
                    e, change = changed(field, row, tile, p, speed)
                    new(tile, p, e + change)
        return body

    def short4(row):
        for tile in range(4):
            speed = rate[row, tile]
            for p in range(ORDERS):
                e, change = changed(a1p, row, tile, p, speed)
                a2.value[row, tile, p] = e + change

    outs = (start_hbm, end_hbm)

    def sends(which):
        return [
            pltpu.make_async_copy(
                result.at[which, half, :, pl.ds(1, ROWS)],
                outs[which].at[0, :, :, :, pl.ds(128 * half, 128)],
                out_sem.at[2 * which + half],
            )
            for half in (0, 1)
        ]

    def send(ends, starts):
        for which, holder in enumerate((starts, ends)):
            @pl.when(tm == holder)
            def _():
                for copy in sends(which):
                    copy.start()

    def write(field, ends, starts):
        @pl.when(jnp.logical_or(tm == ends, tm == starts))
        def _():
            which = jnp.where(tm == ends, 1, 0)
            for zt in (0, 1):
                pieces = []
                for yt in (0, 1):
                    rest = field.value.brick(2 * zt + yt).reshape(ROWS * ORDERS * 8, 128)
                    parts = []
                    for _ in range(2):
                        parts.append(rest.astype(jnp.bfloat16))
                        rest = rest - parts[-1].astype(jnp.float32)
                    pieces.append(parts)
                mixed = None
                for left, right in zip(*pieces):
                    moved = jnp.dot(jnp.concatenate([left, right], axis=1), gather[...], preferred_element_type=jnp.float32)
                    mixed = moved if mixed is None else mixed + moved
                mixed = mixed.reshape(ROWS, ORDERS, 8, 256)
                for row in range(ROWS):
                    for half in (0, 1):
                        result[which, half, :, row + 1, pl.ds(zt, 8, stride=2), :] = mixed[row, :, :, 128 * half : 128 * half + 128]

        send(ends, starts)

    @pl.when(tm == 0)
    def _():
        for half in (0, 1):
            for row in range(ROWS):
                order = cells[0, half, HALO + row] & (ORDERS - 1)
                for p in range(ORDERS):
                    result[0, half, p, row + 1] = jnp.where(order == p, ROOT2, 0.0)

    send(-1, 0)
    unpack(HALO, ROWS)
    pairs(HALO, ROWS // 2, prepare)

    low_late = place < 2

    def split(level, phase, lo, hi):
        reach = by_slice(tm, REACH[level])
        total = jnp.where(reach < 0, 0, ROWS // 2 + reach)
        depth = int(level)
        low = jnp.minimum((depth + reach + 1) // 2, total)
        high = total - jnp.maximum((ROWS - depth + reach) // 2, 0)
        late = jnp.where(low_late, low, high)
        late = jnp.clip(late, 0, total)
        number = jnp.where(phase == 0, total - late, late)
        at_low = jnp.logical_xor(low_late, phase == 0)
        first = HALO - reach + jnp.where(at_low, 0, 2 * (total - number))
        return first, jnp.where(jnp.logical_and(tm >= lo, tm <= hi), number, 0)

    def phases(phase, carry):
        at_low = jnp.logical_xor(low_late, phase == 0)
        for side, (halos, far_halos, hands, far_hands) in enumerate(SIDES):
            @pl.when(at_low if side == 0 else jnp.logical_not(at_low))
            def _():
                halo_received(halos)
                if side == 1:
                    relay(start)
                hand(hands, True, start)
                hand(hands, False, received)
        first = jnp.where(at_low, HALO - 4, HALO + ROWS)
        unpack(first, 4)
        pairs(first, 2, prepare)
        for side, (halos, far_halos, hands, far_hands) in enumerate(SIDES):
            @pl.when(at_low if side == 0 else jnp.logical_not(at_low))
            def _():
                halo_received(far_halos)
                hand(far_hands, True, start)
                hand(far_hands, False, received)

        @pl.when(tm >= 2)
        def _():
            outer = jnp.where(at_low, 0, EXT - 2)
            unpack(outer, 2)
            pairs(outer, 1, prepare)

        pairs(*split("1", phase, 2, 3), level1)
        pairs(*split("1", phase, 0, 1), short1)
        pairs(*split("2", phase, 2, 3), level2)
        pairs(*split("2", phase, 0, 1), short(u0p, a1))

        @pl.when(phase == 1)
        def _():
            write(a1, 0, 1)

        pairs(*split("3", phase, 2, 3), level3)
        pairs(*split("3", phase, 0, 1), short(a1, a1p))
        pairs(*split("4", phase, 2, 3), level4)
        pairs(*split("4", phase, 0, 1), short4)
        return carry

    lax.fori_loop(0, 2, phases, 0)
    write(a2, 1, 2)
    level_of("5", level5)
    write(d3, 2, 3)
    level_of("6", level6)
    write(e4, 3, -1)
    halo(sent)
    relay(sent)
    hand(range(6), True, sent)
    for which in (0, 1):
        for copy in sends(which):
            copy.wait()


def annealing(labels, particles, grain_class, class_energy):
    out = jax.ShapeDtypeStruct((1, ORDERS, ROWS, 16, 256), jnp.float32)
    arguments = [labels, particles, grain_class.reshape(1, -1), class_energy]
    made = pl.pallas_call(
        annealing_kernel,
        out_shape=(out, out),
        in_specs=[pl.BlockSpec(memory_space=pltpu.HBM)] * 4,
        out_specs=[pl.BlockSpec(memory_space=pl.ANY)] * 2,
        scratch_shapes=[
            pltpu.VMEM((2, 2, EXT, 16, 128), jnp.int32),
            pltpu.VMEM((1, 128), jnp.int32),
            pltpu.SMEM((4,), jnp.float32),
            pltpu.VMEM((2, 2, ORDERS, ROWS + 2, 16, 128), jnp.float32),
            pltpu.SemaphoreType.DMA((6,)),
            pltpu.SemaphoreType.DMA((20,)),
            pltpu.SemaphoreType.DMA((10,)),
            pltpu.SemaphoreType.DMA((4,)),
            pltpu.VMEM((256, 256), jnp.bfloat16),
            pltpu.VMEM((256, 256), jnp.bfloat16),
            pltpu.VMEM((EXT, 4, 8, 128), jnp.int32),
            pltpu.VMEM((EXT, 8, 8, 128), jnp.int32),
        ]
        + [pltpu.VMEM((EXT, places, 8, 128), jnp.float32) for places in (FIXED, PLACES, PLACES)],
        compiler_params=pltpu.CompilerParams(
            collective_id=0, has_side_effects=True, vmem_limit_bytes=52 * 1024 * 1024
        ),
        name="annealing",
    )(*(pltpu.with_memory_space_constraint(a, pltpu.HBM) for a in arguments))
    return tuple(part * (1.0 / ROOT2) for part in made)


def solution(mesh):
    placed = (P("space", None, None), P("space", None, None), P(), P())
    return jax.shard_map(
        annealing,
        mesh=mesh,
        in_specs=placed,
        out_specs=(P("tm", None, "space", None, None), P("tm", None, "space", None, None)),
        check_vma=False,
    )
```

```python
import functools
import math

import jax
import jax.numpy as jnp
from jax import lax
from jax.experimental import pallas as pl
from jax.experimental.pallas import tpu as pltpu
from jax.sharding import PartitionSpec as P

MESH = pl.DeviceIdType.MESH
ORDERS = 8
HALO = 6
ROWS = 4
EXT = ROWS + 2 * HALO
FINE_DT = 0.06
ROOT2 = math.sqrt(2.0)

REACH = {
    "1": (1, 3, 4, 5),
    "2": (0, 2, 3, 4),
    "3": (-1, 1, 2, 3),
    "4": (-1, 0, 1, 2),
    "5": (-1, -1, 0, 1),
    "6": (-1, -1, -1, 0),
}


def by_slice(tm, values):
    result = jnp.int32(values[0])
    for index in range(1, len(values)):
        result = jnp.where(tm >= index, jnp.int32(values[index]), result)
    return result


TURN = (1, 127)


def order_of_lanes(across):
    y = lax.broadcasted_iota(jnp.int32, (256, 256), across)
    place = lax.broadcasted_iota(jnp.int32, (256, 256), 1 - across)
    return jnp.where(y == 2 * (place & 127) + (place >> 7), 1.0, 0.0).astype(jnp.bfloat16)


class View:
    def __init__(self, store, first, orders):
        self.store, self.first, self.orders = store, first, orders

    def at(self, index):
        return (index[0], self.first + index[1] * self.orders + (index[2] if self.orders > 1 else 0))

    def __getitem__(self, index):
        return self.store[self.at(index)]

    def __setitem__(self, index, tile):
        self.store[self.at(index)] = tile

    def brick(self, tile):
        return self.store[pl.ds(HALO, ROWS), pl.ds(self.first + tile * self.orders, self.orders)]


class Shelf:
    def __init__(self, store):
        self.store, self.used = store, 0

    def planes(self):
        return self.view(1)

    def field(self):
        return self.view(ORDERS)

    def view(self, orders):
        self.used += 4 * orders
        return View(self.store, self.used - 4 * orders, orders)


FIXED = 4 * (3 + ORDERS)
PLACES = 4 * (ORDERS + 3 * (3 * ORDERS + 1))


class Field:
    def __init__(self, shelf):
        self.value, self.turned, self.term, self.level = shelf.field(), shelf.field(), shelf.field(), shelf.planes()


def around(field, row, tile, order):
    e, beyond = field.value[row, tile, order], field.value[row, tile ^ 2, order]
    along_y = field.value[row, tile ^ 1, order] + field.turned[row, tile, order]
    along_z = beyond + pltpu.roll(beyond, 1 if tile < 2 else 7, 0)
    return e, (along_y + along_z) + (field.value[row - 1, tile, order] + field.value[row + 1, tile, order])


MOVES = (
    (1, 1, 0, 2, 6, 4, 2),
    (-1, 1, 0, 2, 6, 4, 10),
    (2, 3, 0, 1, 8, 2, 0),
    (-2, 3, 0, 1, 6, 2, 14),
    (2, 3, 1, 1, 9, 1, 1),
    (-2, 3, 1, 1, 6, 1, 14),
)
HANDED = ((1, 4, 2, 6), (1, 10, 2, 7), (3, 2, 4, 6), (3, 10, 4, 7), (3, 1, 1, 8), (3, 14, 1, 9))


SIDES = (((0,), (2, 4), (0, 2), (4,)), ((1,), (3, 5), (1, 3), (5,)))


def annealing_kernel(
    lab_hbm, msk_hbm, class_hbm, energy_hbm, start_hbm, end_hbm,
    cells, class_ref, energy_ref, result, in_sem, send_sem, recv_sem, out_sem, deal, gather, code, marks, fixed, store_a, store_b,
):
    tm, me = lax.axis_index("tm"), lax.axis_index("space")
    count = lax.axis_size("space")
    place = lax.rem(me, 4)

    local_copies = [
        pltpu.make_async_copy(
            src.at[:, :, pl.ds(128 * half, 128)], cells.at[k, half, pl.ds(HALO, ROWS)], in_sem.at[2 * k + half]
        )
        for k, src in enumerate((lab_hbm, msk_hbm))
        for half in (0, 1)
    ]
    table_copies = [
        pltpu.make_async_copy(class_hbm, class_ref, in_sem.at[4]),
        pltpu.make_async_copy(energy_hbm, energy_ref, in_sem.at[5]),
    ]
    for copy in local_copies + table_copies:
        copy.start()

    odd = lax.rem(tm, 2) == 1

    def away(distance, holder):
        return holder, lax.rem(me + distance + count, count)

    def crosses(distance):
        return jnp.logical_or(place + distance < 0, place + distance > 3)

    def across(distance):
        sends = jnp.logical_and(tm == 1, crosses(distance))
        return jnp.logical_and(sends, place != 1) if distance == -2 else sends

    def greet(device):
        pl.semaphore_signal(barrier, inc=1, device_id=device, device_id_type=MESH)

    barrier = pltpu.get_barrier_semaphore()
    targets = 1
    for distance in (1, -1, 2, -2):
        one = abs(distance) == 1
        greets = odd if one else tm == 3
        if distance == 2:
            greets = jnp.logical_and(greets, place != 3)
        pl.when(greets)(
            functools.partial(greet, away(distance, jnp.where(crosses(distance), 1, tm)))
        )
        straight = jnp.where(crosses(distance), tm == 1, tm >= (1 if one else 3))
        if not one:
            straight = jnp.logical_and(straight, tm == 3)
        targets = targets + jnp.where(straight, 1, 0) + jnp.where(across(distance), 1, 0)

    @pl.when(jnp.logical_not(odd))
    def _():
        greet((tm + 1, me))

    def moved(m, over):
        distance, _, array, arrays, first, rows, there = MOVES[m]
        return pltpu.make_async_remote_copy(
            src_ref=cells.at[pl.ds(array, arrays), :, pl.ds(first, rows)],
            dst_ref=cells.at[pl.ds(array, arrays), :, pl.ds(there, rows)],
            send_sem=send_sem.at[10 * over + m],
            recv_sem=recv_sem.at[m],
            device_id=away(distance, 3 if over else tm),
            device_id_type=MESH,
        )

    def halo(act):
        for m, (distance, least, *_) in enumerate(MOVES):
            pl.when(across(distance))(functools.partial(act, moved(m, 1)))
        for m, (distance, least, *_) in enumerate(MOVES):
            inside = jnp.logical_or(tm == 1, jnp.logical_not(crosses(distance)))
            wanted = jnp.logical_and(jnp.logical_and(odd, tm >= least), inside)
            pl.when(wanted)(functools.partial(act, moved(m, 0)))

    def relay(act):
        for m in (3, 5):
            _, _, array, arrays, first, rows, there = MOVES[m]
            copy = pltpu.make_async_remote_copy(
                src_ref=cells.at[pl.ds(array, arrays), :, pl.ds(first + ROWS, rows)],
                dst_ref=cells.at[pl.ds(array, arrays), :, pl.ds(there, rows)],
                send_sem=send_sem.at[13 + m],
                recv_sem=recv_sem.at[m],
                device_id=away(-1, 3),
                device_id_type=MESH,
            )
            pl.when(jnp.logical_and(tm == 1, place == 0))(functools.partial(act, copy))

    def halo_received(moves):
        for m in moves:
            pl.when(jnp.logical_and(odd, tm >= MOVES[m][1]))(moved(m, 0).wait_recv)

    def hand(copies, sending, act):
        for h in copies:
            holder, first, rows, sem = HANDED[h]
            copy = pltpu.make_async_remote_copy(
                src_ref=cells.at[:, :, pl.ds(first, rows)],
                dst_ref=cells.at[:, :, pl.ds(first, rows)],
                send_sem=send_sem.at[sem],
                recv_sem=recv_sem.at[sem],
                device_id=(holder - 1, me),
                device_id_type=MESH,
            )
            pl.when(tm == (holder if sending else holder - 1))(functools.partial(act, copy))

    start, sent, received = (lambda copy: copy.start()), (lambda copy: copy.wait_send()), (lambda copy: copy.wait_recv())

    for row in (0, EXT - 1):
        for half in (0, 1):
            cells[1, half, row] = jnp.zeros((16, 128), jnp.int32)
    for copy in local_copies:
        copy.wait()

    early = jnp.logical_and(tm == 1, place == 0)

    def depart():
        pl.semaphore_wait(barrier, targets)
        halo(start)

    pl.when(jnp.logical_and(odd, jnp.logical_not(early)))(depart)

    for copy in table_copies:
        copy.wait()
    deal[...] = order_of_lanes(0)
    gather[...] = order_of_lanes(1)
    classes = jnp.broadcast_to(class_ref[...], (8, 128))
    table = jnp.full((8, 128), energy_ref[0], jnp.float32)
    for kind in range(1, 4):
        table = jnp.where(classes == kind, energy_ref[kind], table)

    shelf = Shelf(fixed)
    rate, base, weight, drive = shelf.planes(), shelf.planes(), shelf.planes(), shelf.field()
    shelf = Shelf(store_a)
    held_a, (a1, c1p, c2) = shelf.field(), [Field(shelf) for _ in range(3)]
    shelf = Shelf(store_b)
    held_b, (a1p, b2, c2p) = shelf.field(), [Field(shelf) for _ in range(3)]
    a2, b2p, b3 = a1, c1p, c2
    e4 = a1
    u0p, c1 = d3, b3p = a1p, b2

    def unpack(first, rows):
        for zt in (0, 1):
            found = None
            for half in (0, 1):
                there = (pl.ds(first, rows), pl.ds(zt, 8, stride=2))
                both = cells[0, half, *there] + 128 * cells[1, half, *there]
                part = jnp.dot(
                    both.astype(jnp.float32).reshape(rows * 8, 128).astype(jnp.bfloat16),
                    deal[pl.ds(128 * half, 128), :],
                    preferred_element_type=jnp.float32,
                )
                found = part if found is None else found + part
            found = found.astype(jnp.int32).reshape(rows, 8, 256)
            for yt in (0, 1):
                code[pl.ds(first, rows), 2 * zt + yt] = found[:, :, 128 * yt : 128 * yt + 128]

    def prepare(row):
        for tile in range(4):
            both = code[row, tile]
            label = both & 127
            rate[row, tile] = jnp.where(both > 127, 0.25 * FINE_DT, FINE_DT)
            stored = jnp.take_along_axis(table, label, axis=1, mode="promise_in_bounds")
            base[row, tile] = 1.5 * stored + 5.0
            weight[row, tile] = ROOT2 * stored + ROOT2 * 6.0
            order = both & (ORDERS - 1)
            mark = jnp.left_shift(1, 4 * order)
            marks[row, tile] = mark
            marks[row, 4 + (tile ^ 1)] = pltpu.roll(mark, TURN[1 - (tile & 1)], 1)
            for p in range(ORDERS):
                drive[row, tile, p] = jnp.where(order == p, stored, 0.0)

    def pairs(first, count, body):
        def once(k, carry):
            body(first + 2 * k)
            body(first + 2 * k + 1)
            return carry
        lax.fori_loop(0, count, once, 0)

    def level_of(name, body):
        reach = by_slice(tm, REACH[name])
        pairs(HALO - reach, jnp.where(reach < 0, 0, ROWS // 2 + reach), body)

    class Made:
        def __init__(self, field, row):
            self.field, self.row, self.total = field, row, [None] * 4

        def __call__(self, tile, p, value):
            self.field.value[self.row, tile, p] = value
            self.field.turned[self.row, tile ^ 1, p] = pltpu.roll(value, TURN[1 - (tile & 1)], 1)
            part = value * value - drive[self.row, tile, p]
            self.field.term[self.row, tile, p] = part
            self.total[tile] = part if p == 0 else self.total[tile] + part
            if p == ORDERS - 1:
                self.field.level[self.row, tile] = 1.5 * self.total[tile] + base[self.row, tile]

    def force(field, row, tile, p):
        e, beside = around(field, row, tile, p)
        return e, beside + e * (field.term[row, tile, p] - field.level[row, tile])

    def changed(field, row, tile, p, speed):
        e, push = force(field, row, tile, p)
        return e, speed * push

    def level1(row):
        new_u0p, new_c1 = Made(u0p, row), Made(c1, row)
        for tile in range(4):
            beside = counts(row, tile)
            order = code[row, tile] & (ORDERS - 1)
            speed = rate[row, tile]
            quick, own = ROOT2 * speed, ROOT2 - speed * weight[row, tile]
            for p in range(ORDERS):
                mine = order == p
                share = quick * (jnp.right_shift(beside, 4 * p) & 7).astype(jnp.float32)
                half = share + jnp.where(mine, own, 0.0)
                new_u0p(tile, p, half)
                new_c1(tile, p, (half + half) - jnp.where(mine, ROOT2, 0.0))

    def level2(row):
        new_a1, new_c1p, new_c2 = Made(a1, row), Made(c1p, row), Made(c2, row)
        for tile in range(4):
            speed = rate[row, tile]
            for p in range(ORDERS):
                e, change = changed(u0p, row, tile, p, speed)
                new_a1(tile, p, e + change)
            for p in range(ORDERS):
                e, change = changed(c1, row, tile, p, speed)
                half = e + change
                new_c1p(tile, p, half)
                new_c2(tile, p, half + change)
                held_a[row, tile, p] = change

    def level3(row):
        new_a1p, new_b2, new_c2p = Made(a1p, row), Made(b2, row), Made(c2p, row)
        for tile in range(4):
            speed = rate[row, tile]
            for p in range(ORDERS):
                jump = changed(c1p, row, tile, p, speed)[1] - held_a[row, tile, p]
                e, change = changed(a1, row, tile, p, speed)
                half = e + change
                new_a1p(tile, p, half)
                new_b2(tile, p, half + (change + jump))
            for p in range(ORDERS):
                e, change = changed(c2, row, tile, p, speed)
                new_c2p(tile, p, e + change)
                held_b[row, tile, p] = change

    def level4(row):
        new_a2, new_b2p, new_b3 = Made(a2, row), Made(b2p, row), Made(b3, row)
        for tile in range(4):
            speed = rate[row, tile]
            for p in range(ORDERS):
                e, change = changed(a1p, row, tile, p, speed)
                new_a2(tile, p, e + change)
            for p in range(ORDERS):
                jump = changed(c2p, row, tile, p, speed)[1] - held_b[row, tile, p]
                e, push = force(b2, row, tile, p)
                change = speed * push
                half = e + change
                new_b2p(tile, p, half)
                new_b3(tile, p, half + (change + jump))
                held_a[row, tile, p] = push

    def level5(row):
        new_d3, new_b3p = Made(d3, row), Made(b3p, row)
        for tile in range(4):
            speed = rate[row, tile]
            for p in range(ORDERS):
                jump = force(b2p, row, tile, p)[1] - held_a[row, tile, p]
                e, push = force(a2, row, tile, p)
                new_d3(tile, p, e + speed * (push + (push + jump)))
            for p in range(ORDERS):
                e, push = force(b3, row, tile, p)
                new_b3p(tile, p, e + speed * push)
                held_b[row, tile, p] = push

    def level6(row):
        for tile in range(4):
            speed = rate[row, tile]
            for p in range(ORDERS):
                jump = force(b3p, row, tile, p)[1] - held_b[row, tile, p]
                e, push = force(d3, row, tile, p)
                e4.value[row, tile, p] = e + speed * (push + (push + jump))

    def counts(row, tile):
        beyond = marks[row, tile ^ 2]
        beside = marks[row, tile ^ 1] + marks[row, 4 + tile] + beyond + pltpu.roll(beyond, 1 if tile < 2 else 7, 0)
        return beside + marks[row - 1, tile] + marks[row + 1, tile]

    def short1(row):
        new_u0p = Made(u0p, row)
        for tile in range(4):
            beside, order, speed = counts(row, tile), code[row, tile] & (ORDERS - 1), rate[row, tile]
            quick, own = ROOT2 * speed, ROOT2 - speed * weight[row, tile]
            for p in range(ORDERS):
                share = quick * (jnp.right_shift(beside, 4 * p) & 7).astype(jnp.float32)
                new_u0p(tile, p, share + jnp.where(order == p, own, 0.0))

    def short(field, made):
        def body(row):
            new = Made(made, row)
            for tile in range(4):
                speed = rate[row, tile]
                for p in range(ORDERS):
                    e, change = changed(field, row, tile, p, speed)
                    new(tile, p, e + change)
        return body

    def short4(row):
        for tile in range(4):
            speed = rate[row, tile]
            for p in range(ORDERS):
                e, change = changed(a1p, row, tile, p, speed)
                a2.value[row, tile, p] = e + change

    outs = (start_hbm, end_hbm)

    def sends(which):
        return [
            pltpu.make_async_copy(
                result.at[which, half, :, pl.ds(1, ROWS)],
                outs[which].at[0, :, :, :, pl.ds(128 * half, 128)],
                out_sem.at[2 * which + half],
            )
            for half in (0, 1)
        ]

    def send(ends, starts):
        for which, holder in enumerate((starts, ends)):
            @pl.when(tm == holder)
            def _():
                for copy in sends(which):
                    copy.start()

    def write(field, ends, starts):
        @pl.when(jnp.logical_or(tm == ends, tm == starts))
        def _():
            which = jnp.where(tm == ends, 1, 0)
            for zt in (0, 1):
                pieces = []
                for yt in (0, 1):
                    rest = field.value.brick(2 * zt + yt).reshape(ROWS * ORDERS * 8, 128)
                    parts = []
                    for _ in range(2):
                        parts.append(rest.astype(jnp.bfloat16))
                        rest = rest - parts[-1].astype(jnp.float32)
                    pieces.append(parts)
                mixed = None
                for left, right in zip(*pieces):
                    moved = jnp.dot(jnp.concatenate([left, right], axis=1), gather[...], preferred_element_type=jnp.float32)
                    mixed = moved if mixed is None else mixed + moved
                mixed = mixed.reshape(ROWS, ORDERS, 8, 256)
                for row in range(ROWS):
                    for half in (0, 1):
                        result[which, half, :, row + 1, pl.ds(zt, 8, stride=2), :] = mixed[row, :, :, 128 * half : 128 * half + 128]

        send(ends, starts)

    @pl.when(tm == 0)
    def _():
        for half in (0, 1):
            for row in range(ROWS):
                order = cells[0, half, HALO + row] & (ORDERS - 1)
                for p in range(ORDERS):
                    result[0, half, p, row + 1] = jnp.where(order == p, ROOT2, 0.0)

    send(-1, 0)
    unpack(HALO, ROWS)
    pairs(HALO, ROWS // 2, prepare)
    pl.when(early)(depart)

    low_late = place < 2

    def split(level, phase, lo, hi):
        reach = by_slice(tm, REACH[level])
        total = jnp.where(reach < 0, 0, ROWS // 2 + reach)
        depth = int(level)
        low = jnp.minimum((depth + reach + 1) // 2, total)
        high = total - jnp.maximum((ROWS - depth + reach) // 2, 0)
        late = jnp.where(low_late, low, high)
        late = jnp.clip(late, 0, total)
        number = jnp.where(phase == 0, total - late, late)
        at_low = jnp.logical_xor(low_late, phase == 0)
        first = HALO - reach + jnp.where(at_low, 0, 2 * (total - number))
        return first, jnp.where(jnp.logical_and(tm >= lo, tm <= hi), number, 0)

    def phases(phase, carry):
        at_low = jnp.logical_xor(low_late, phase == 0)
        for side, (halos, far_halos, hands, far_hands) in enumerate(SIDES):
            @pl.when(at_low if side == 0 else jnp.logical_not(at_low))
            def _():
                halo_received(halos)
                if side == 1:
                    relay(start)
                hand(hands, True, start)
                hand(hands, False, received)
        first = jnp.where(at_low, HALO - 4, HALO + ROWS)
        unpack(first, 4)
        pairs(first, 2, prepare)
        for side, (halos, far_halos, hands, far_hands) in enumerate(SIDES):
            @pl.when(at_low if side == 0 else jnp.logical_not(at_low))
            def _():
                halo_received(far_halos)
                hand(far_hands, True, start)
                hand(far_hands, False, received)

        @pl.when(tm >= 2)
        def _():
            outer = jnp.where(at_low, 0, EXT - 2)
            unpack(outer, 2)
            pairs(outer, 1, prepare)

        pairs(*split("1", phase, 2, 3), level1)
        pairs(*split("1", phase, 0, 1), short1)
        pairs(*split("2", phase, 2, 3), level2)
        pairs(*split("2", phase, 0, 1), short(u0p, a1))

        @pl.when(phase == 1)
        def _():
            write(a1, 0, 1)

        pairs(*split("3", phase, 2, 3), level3)
        pairs(*split("3", phase, 0, 1), short(a1, a1p))
        pairs(*split("4", phase, 2, 3), level4)
        pairs(*split("4", phase, 0, 1), short4)
        return carry

    lax.fori_loop(0, 2, phases, 0)
    write(a2, 1, 2)
    level_of("5", level5)
    write(d3, 2, 3)
    level_of("6", level6)
    write(e4, 3, -1)
    halo(sent)
    relay(sent)
    hand(range(6), True, sent)
    for which in (0, 1):
        for copy in sends(which):
            copy.wait()


def annealing(labels, particles, grain_class, class_energy):
    out = jax.ShapeDtypeStruct((1, ORDERS, ROWS, 16, 256), jnp.float32)
    arguments = [labels, particles, grain_class.reshape(1, -1), class_energy]
    made = pl.pallas_call(
        annealing_kernel,
        out_shape=(out, out),
        in_specs=[pl.BlockSpec(memory_space=pltpu.HBM)] * 4,
        out_specs=[pl.BlockSpec(memory_space=pl.ANY)] * 2,
        scratch_shapes=[
            pltpu.VMEM((2, 2, EXT, 16, 128), jnp.int32),
            pltpu.VMEM((1, 128), jnp.int32),
            pltpu.SMEM((4,), jnp.float32),
            pltpu.VMEM((2, 2, ORDERS, ROWS + 2, 16, 128), jnp.float32),
            pltpu.SemaphoreType.DMA((6,)),
            pltpu.SemaphoreType.DMA((20,)),
            pltpu.SemaphoreType.DMA((10,)),
            pltpu.SemaphoreType.DMA((4,)),
            pltpu.VMEM((256, 256), jnp.bfloat16),
            pltpu.VMEM((256, 256), jnp.bfloat16),
            pltpu.VMEM((EXT, 4, 8, 128), jnp.int32),
            pltpu.VMEM((EXT, 8, 8, 128), jnp.int32),
        ]
        + [pltpu.VMEM((EXT, places, 8, 128), jnp.float32) for places in (FIXED, PLACES, PLACES)],
        compiler_params=pltpu.CompilerParams(
            collective_id=0, has_side_effects=True, vmem_limit_bytes=52 * 1024 * 1024
        ),
        name="annealing",
    )(*(pltpu.with_memory_space_constraint(a, pltpu.HBM) for a in arguments))
    return tuple(part * (1.0 / ROOT2) for part in made)


def solution(mesh):
    placed = (P("space", None, None), P("space", None, None), P(), P())
    return jax.shard_map(
        annealing,
        mesh=mesh,
        in_specs=placed,
        out_specs=(P("tm", None, "space", None, None), P("tm", None, "space", None, None)),
        check_vma=False,
    )
```
